512 devices in a mesh: dp: 16 (over x_lo, y), ctx: 32 (over x_hi, z, core).
Axes of the slice: x: 4 (x_hi: 2, x_lo: 2; x = x_hi * 2 + x_lo), y: 8, z: 8, core: 2. Of those that a mesh axis runs over, the one named last changes fastest.
Arguments:
- queries: bfloat16 [16, 4096, 1024], P('dp', 'ctx'), may hold values from -6 to 6
- key_states: bfloat16 [16, 4096, 128], P('dp', 'ctx'), may hold values from -6 to 6
- value_states: bfloat16 [16, 4096, 128], P('dp', 'ctx'), may hold values from -6 to 6
- doc_start: int32 [16, 4096], P('dp', 'ctx'), may hold values from 0 to 4095, as said below
- move_plan: int32 [32, 8], P('ctx'), may hold values from 0 to 15, as said below
- out_grad: bfloat16 [16, 4096, 1024], P('dp', 'ctx'), may hold values from -6 to 6
Outputs:
- attn_moved: bfloat16 [16, 4096, 1024], P('dp', 'ctx')
- query_grad: bfloat16 [16, 4096, 1024], P('dp', 'ctx')
- key_grad: bfloat16 [16, 4096, 128], P('dp', 'ctx')
- value_grad: bfloat16 [16, 4096, 128], P('dp', 'ctx')
The draws below stay inside these ranges and needn't reach their ends.
Inputs may be any that keep to these rules, and one draw needn't show every extreme that they name: doc_start[g, 0] = 0; doc_start[g, i] <= i; doc_start[g, i] is either i or doc_start[g, i - 1]. `move_plan`: the 8 values of each row are distinct.
All inputs are finite; a program needn't handle non-finite values.
Results may differ from the reference program's by a relative error of at most 0.03.
Values may be sent and summed in bfloat16 or wider, within the bound.
A program may use at most 64 MiB of HBM per device.

```python
import math
import jax
import jax.numpy as jnp
from jax import lax

HEADS = 8
HDIM = 128
TOK_DEV = 128
GROUPS = 16
PIECES = 32
SEQ = 4096
SLOTS = 8


def boundary_marks(key):
    key = jax.random.fold_in(key, 71)
    first_key, second_key = jax.random.split(key, 2)
    positions = jnp.arange(SEQ, dtype=jnp.int32)[None, :]
    dice_rolls = jax.random.randint(first_key, (GROUPS, SEQ), 0, 8 * TOK_DEV)
    long_end = jax.random.randint(second_key, (GROUPS, 1), SEQ * 5 // 8, SEQ * 7 // 8)
    boundary = jnp.where(positions < long_end, False, dice_rolls < 32)
    boundary = boundary | (positions == 0) | (positions == long_end) | (positions == SEQ - 1)
    return boundary


def draw_doc_start(key, part):
    boundary = boundary_marks(key)
    positions = jnp.broadcast_to(jnp.arange(SEQ, dtype=jnp.int32)[None, :], (GROUPS, SEQ))
    return lax.cummax(jnp.where(boundary, positions, 0), axis=1).astype(jnp.int32)


def draw_queries(key, part):
    key = jax.random.fold_in(key, 5)
    return jnp.clip(jax.random.normal(key, (GROUPS, SEQ, HEADS * HDIM), jnp.float32), -6.0, 6.0).astype(jnp.bfloat16)


def draw_key_states(key, part):
    key = jax.random.fold_in(key, 6)
    return jnp.clip(jax.random.normal(key, (GROUPS, SEQ, HDIM), jnp.float32), -6.0, 6.0).astype(jnp.bfloat16)


def shared_part(key, level):
    boundary = boundary_marks(key)
    positions = jnp.broadcast_to(jnp.arange(SEQ, dtype=jnp.int32)[None, :], (GROUPS, SEQ))
    starts = lax.cummax(jnp.where(boundary, positions, 0), axis=1)
    inside = (starts == 0) & (positions >= SEQ // 2)
    sign_key = jax.random.fold_in(key, 113)
    column_signs = jnp.where(jax.random.randint(sign_key, (GROUPS, 1, HEADS * HDIM), 0, 2) == 0, -1.0, 1.0)
    return jnp.where(inside[:, :, None], level * column_signs, 0.0).astype(jnp.float32)


def draw_out_grad(key, part):
    common = shared_part(key, 2.0)
    key = jax.random.fold_in(key, 9)
    noise = jnp.clip(jax.random.normal(key, (GROUPS, SEQ, HEADS * HDIM), jnp.float32), -4.0, 4.0)
    return (noise + common).astype(jnp.bfloat16)


def first_slots(row_key):
    return jax.random.permutation(row_key, GROUPS)[:SLOTS]


def draw_move_plan(key, part):
    key = jax.random.fold_in(key, 7)
    row_keys = jax.random.split(key, PIECES)
    return jax.vmap(first_slots)(row_keys).astype(jnp.int32)


def block_scale(own_key, dims, cuts, smallest, largest):
    loudness = 1.0
    for dim, blocks in cuts:
        draws = jax.random.uniform(jax.random.fold_in(jax.random.fold_in(own_key, 6), dim), (blocks,), jnp.float32, smallest / len(cuts), largest / len(cuts))
        loudness = loudness * jnp.repeat(jnp.exp(draws), dims[dim] // blocks).reshape((-1,) + (1,) * (len(dims) - 1 - dim))
    return loudness


def gaussian(stream_key, extent, deviation, most, cuts=(), kind=jnp.bfloat16):
    values = jax.random.normal(stream_key, extent, jnp.float32) * deviation
    if len(cuts) > 0:
        values = block_scale(stream_key, extent, cuts, -0.22, 0.18) * values
    return jnp.clip(values, min=-most, max=most).astype(kind)


def setup_inputs(seed: int = 0) -> dict:
    splits = jax.random.split(jax.random.key(seed), 7)
    queries = draw_queries(jax.random.fold_in(splits[6], 71), 0)
    key_states = draw_key_states(jax.random.fold_in(splits[6], 71), 0)
    value_states = gaussian(splits[2], (GROUPS, SEQ, HDIM), 1.0, 6.0, ((0, 16), (1, 32)))
    doc_start = draw_doc_start(jax.random.fold_in(splits[6], 71), 0)
    move_plan = draw_move_plan(jax.random.fold_in(splits[6], 71), 0)
    out_grad = draw_out_grad(jax.random.fold_in(splits[6], 71), 0)
    return dict(queries=queries, key_states=key_states, value_states=value_states, doc_start=doc_start, move_plan=move_plan, out_grad=out_grad)


MASKED_SCORE = -1e+30

def reference(queries, key_states, value_states, doc_start, move_plan, out_grad):
    score_scale = 1.0 / math.sqrt(HDIM)
    block_rows = TOK_DEV // SLOTS
    token_ids = jnp.arange(SEQ, dtype=jnp.int32)
    token_shift = move_plan[token_ids // TOK_DEV, token_ids % TOK_DEV // block_rows]
    group_ids = jnp.arange(GROUPS, dtype=jnp.int32)
    home_grad = out_grad[jnp.mod(group_ids[:, None] + token_shift[None, :], GROUPS), token_ids[None, :]]

    def group_pass(inputs):
        query_all, key_all, value_all, start_all, grad_all = inputs
        key_wide = key_all.astype(jnp.float32)
        value_wide = value_all.astype(jnp.float32)

        def block_pass(totals, block_index):
            first_row = block_index * TOK_DEV
            query_rows = lax.dynamic_slice_in_dim(query_all, first_row, TOK_DEV, 0)
            query_rows = query_rows.reshape(TOK_DEV * HEADS, HDIM).astype(jnp.float32)
            grad_rows = lax.dynamic_slice_in_dim(grad_all, first_row, TOK_DEV, 0)
            grad_wide = grad_rows.reshape(TOK_DEV * HEADS, HDIM).astype(jnp.float32)
            starts = lax.dynamic_slice_in_dim(start_all, first_row, TOK_DEV, 0)
            positions = first_row + jnp.arange(TOK_DEV, dtype=jnp.int32)
            visible = (token_ids[None, :] >= starts[:, None]) & (token_ids[None, :] <= positions[:, None])
            raw_scores = jnp.dot(query_rows, key_wide.T, preferred_element_type=jnp.float32) * score_scale
            masked = jnp.where(visible[:, None, :], raw_scores.reshape(TOK_DEV, HEADS, SEQ), MASKED_SCORE)
            row_max = lax.optimization_barrier(jnp.max(masked, axis=2, keepdims=True))
            row_total = lax.optimization_barrier(jnp.sum(jnp.exp(masked - row_max), axis=2, keepdims=True))
            weights = (jnp.exp(masked - row_max) / row_total).reshape(TOK_DEV * HEADS, SEQ)
            rounded = lax.optimization_barrier(weights.astype(jnp.bfloat16)).astype(jnp.float32)
            attended = jnp.dot(rounded, value_wide, preferred_element_type=jnp.float32).astype(jnp.bfloat16)
            attended_wide = lax.optimization_barrier(attended).astype(jnp.float32)
            grad_dot = lax.optimization_barrier(jnp.sum(grad_wide * attended_wide, axis=1, keepdims=True))
            grad_weights = jnp.dot(grad_wide, value_wide.T, preferred_element_type=jnp.float32)
            grad_scores = (weights * (grad_weights - grad_dot) * score_scale).astype(jnp.bfloat16)
            grad_scores = lax.optimization_barrier(grad_scores).astype(jnp.float32)
            query_grad = jnp.dot(grad_scores, key_wide, preferred_element_type=jnp.float32).astype(jnp.bfloat16)
            key_part = jnp.dot(grad_scores.T, query_rows, preferred_element_type=jnp.float32)
            value_part = jnp.dot(rounded.T, grad_wide, preferred_element_type=jnp.float32)
            partial_value = jnp.concatenate([key_part, value_part], axis=1).astype(jnp.bfloat16)
            partial_value = lax.optimization_barrier(partial_value).astype(jnp.float32)
            outputs = (attended.reshape(TOK_DEV, HEADS * HDIM), query_grad.reshape(TOK_DEV, HEADS * HDIM))
            return (totals + partial_value, outputs)
        start_totals = jnp.zeros((SEQ, 2 * HDIM), jnp.float32)
        totals, (attended_all, query_all_grad) = lax.scan(block_pass, start_totals, jnp.arange(PIECES, dtype=jnp.int32))
        key_grad = totals[:, :HDIM].astype(jnp.bfloat16)
        value_grad = totals[:, HDIM:].astype(jnp.bfloat16)
        return (attended_all.reshape(SEQ, HEADS * HDIM), query_all_grad.reshape(SEQ, HEADS * HDIM), key_grad, value_grad)
    attended, query_grad, key_grad, value_grad = lax.map(group_pass, (queries, key_states, value_states, doc_start, home_grad))
    attn_moved = attended[jnp.mod(group_ids[:, None] - token_shift[None, :], GROUPS), token_ids[None, :]]
    return (attn_moved, query_grad, key_grad, value_grad)
```

```python
import functools
import math

import jax
import jax.numpy as jnp
from jax import lax
from jax.experimental import pallas as pl
from jax.experimental.pallas import tpu as pltpu
from jax.sharding import PartitionSpec as P

HDIM = 128
MASKED = -1e30
MESH = pl.DeviceIdType.MESH
VMEM_LIMIT = 56 * 1024 * 1024
CORES = 2
RING = 8


def place():
    ctx = lax.axis_index("ctx")
    group = lax.axis_index("dp")
    chip = ctx // CORES
    return group, ctx, chip // RING, chip % RING, ctx % CORES


def ctx_of(plane, z, core):
    return (plane * RING + z) * CORES + core


def remote(src, dst, send_sem, recv_sem, **axes):
    return pltpu.make_async_remote_copy(
        src_ref=src, dst_ref=dst, send_sem=send_sem, recv_sem=recv_sem,
        device_id=axes, device_id_type=MESH,
    )


def greet(group, plane, z, core, groups):
    barrier = pltpu.get_barrier_semaphore()

    def hello(**axes):
        pl.semaphore_signal(barrier, inc=1, device_id=axes, device_id_type=MESH)

    def dp_peer(s, carry):
        hello(dp=(group + s) % groups)
        return carry

    def z_peer(s, carry):
        hello(ctx=ctx_of(plane, (z + s) % RING, core))
        return carry

    lax.fori_loop(1, groups, dp_peer, 0)
    lax.fori_loop(1, RING, z_peer, 0)
    hello(ctx=ctx_of(1 - plane, z, core))
    hello(ctx=ctx_of(plane, z, 1 - core))
    pl.semaphore_wait(barrier, groups - 1 + RING - 1 + 2)


def slot_of(plan_ref, s, slots):
    found = jnp.int32(0)
    for t in range(slots):
        found = jnp.where(plan_ref[0, t] == s, jnp.int32(t), found)
    return found


def gather_kernel(groups, slots, k_ref, v_ref, grad_ref, plan_ref, kv_ref, home_ref,
                  stage, landed, send_z, send_x, send_s, recv_kv, send_g, recv_g):
    group, ctx, plane, z, core = place()
    greet(group, plane, z, core, groups)
    kv_ref[ctx, :, :HDIM] = k_ref[0]
    kv_ref[ctx, :, HDIM:] = v_ref[0]

    def z_copy(s):
        return remote(kv_ref.at[ctx], kv_ref.at[ctx], send_z.at[s], recv_kv.at[ctx],
                      ctx=ctx_of(plane, (z + s) % RING, core))

    def x_copy(s):
        block = ctx_of(plane, (z + RING - s) % RING, core)
        return remote(kv_ref.at[block], kv_ref.at[block], send_x.at[s], recv_kv.at[block],
                      ctx=ctx_of(1 - plane, z, core))

    def s_copy(owner, s):
        block = ctx_of(owner, (z + RING - s) % RING, core)
        return remote(kv_ref.at[block], kv_ref.at[block], send_s.at[owner * RING + s],
                      recv_kv.at[block], ctx=ctx_of(plane, z, 1 - core))

    def g_copy(s):
        return remote(stage.at[s], landed.at[s], send_g.at[s], recv_g.at[s],
                      dp=(group + groups - s) % groups)

    def arrived(block):
        remote(kv_ref.at[block], kv_ref.at[block], send_z.at[0], recv_kv.at[block],
               ctx=ctx_of(plane, z, 1 - core)).wait_recv()

    def z_start(s, carry):
        @pl.when((plane == 0) | (z + s < RING))
        def _():
            z_copy(s).start()
        return carry

    lax.fori_loop(1, RING, z_start, 0)

    @pl.when(plane == 0)
    def _():
        x_copy(0).start()

    s_copy(plane, 0).start()

    for s in range(groups):
        block = grad_ref[slot_of(plan_ref, s, slots)]
        if s == 0:
            landed[0] = block
        else:
            stage[s] = block

    def g_start(s, carry):
        g_copy(s).start()
        return carry

    lax.fori_loop(1, groups, g_start, 0)

    def z_land(s, carry):
        @pl.when((plane == 0) | (z >= s))
        def _():
            arrived(ctx_of(plane, (z + RING - s) % RING, core))

            @pl.when(plane == 0)
            def _():
                x_copy(s).start()

            s_copy(plane, s).start()
        return carry

    lax.fori_loop(1, RING, z_land, 0)

    @pl.when(plane == 1)
    def _():
        def x_land(s, carry):
            arrived(ctx_of(0, (z + RING - s) % RING, core))
            s_copy(0, s).start()
            return carry

        lax.fori_loop(0, RING, x_land, 0)

    def sib_land(s, carry):
        @pl.when((plane == 0) | (z >= s))
        def _():
            arrived(ctx_of(plane, (z + RING - s) % RING, 1 - core))
        return carry

    lax.fori_loop(0, RING, sib_land, 0)

    @pl.when(plane == 1)
    def _():
        def sib_x(s, carry):
            arrived(ctx_of(0, (z + RING - s) % RING, 1 - core))
            return carry

        lax.fori_loop(0, RING, sib_x, 0)

    def g_land(s, carry):
        g_copy(s).wait_recv()
        return carry

    lax.fori_loop(1, groups, g_land, 0)
    for t in range(slots):
        home_ref[t] = landed[plan_ref[0, t]]

    def g_left(s, carry):
        g_copy(s).wait_send()
        return carry

    lax.fori_loop(1, groups, g_left, 0)

    def z_left(s, carry):
        @pl.when((plane == 0) | (z + s < RING))
        def _():
            z_copy(s).wait_send()
        return carry

    lax.fori_loop(1, RING, z_left, 0)

    def own_left(s, carry):
        @pl.when(plane == 0)
        def _():
            x_copy(s).wait_send()

        @pl.when((plane == 0) | (z >= s))
        def _():
            s_copy(plane, s).wait_send()

        @pl.when(plane == 1)
        def _():
            s_copy(0, s).wait_send()
        return carry

    lax.fori_loop(0, RING, own_left, 0)


def scatter_kernel(groups, slots, attn_ref, part_ref, plan_ref, moved_ref, kg_ref, vg_ref,
                   stage, landed, sib, pair, xbuf, zbuf,
                   send_s, recv_s, send_x, recv_x, send_z, recv_z, send_g, recv_g):
    group, ctx, plane, z, core = place()
    greet(group, plane, z, core, groups)

    def s_copy(owner):
        return remote(part_ref.at[1 - core, owner], sib.at[owner], send_s.at[owner],
                      recv_s.at[owner], ctx=ctx_of(plane, z, 1 - core))

    def x_copy(s):
        spot = (z + s) % RING
        return remote(pair.at[0, spot], xbuf.at[spot], send_x.at[spot], recv_x.at[spot],
                      ctx=ctx_of(1 - plane, z, core))

    def z_copy(s):
        spot = (z + s) % RING
        return remote(pair.at[plane, spot], zbuf.at[z], send_z.at[s], recv_z.at[z],
                      ctx=ctx_of(plane, spot, core))

    def z_arrived(source):
        remote(zbuf.at[source], zbuf.at[source], send_z.at[0], recv_z.at[source],
               ctx=ctx_of(plane, source, core)).wait_recv()

    def g_copy(s):
        return remote(stage.at[s], landed.at[s], send_g.at[s], recv_g.at[s],
                      dp=(group + s) % groups)

    s_copy(0).start()

    @pl.when(plane == 1)
    def _():
        s_copy(1).start()

    for s in range(groups):
        block = attn_ref[slot_of(plan_ref, s, slots)]
        if s == 0:
            landed[0] = block
        else:
            stage[s] = block

    def g_start(s, carry):
        g_copy(s).start()
        return carry

    lax.fori_loop(1, groups, g_start, 0)

    def add(a, b):
        return (a.astype(jnp.float32) + b.astype(jnp.float32)).astype(jnp.bfloat16)

    s_copy(0).wait_recv()

    def pair_zero(s, carry):
        spot = (z + s) % RING
        pair[0, spot] = add(part_ref[core, 0, spot], sib[0, spot])

        @pl.when(plane == 1)
        def _():
            x_copy(s).start()
        return carry

    lax.fori_loop(0, RING, pair_zero, 0)

    @pl.when(plane == 1)
    def _():
        s_copy(1).wait_recv()

        def pair_one(s, carry):
            pair[1, s] = add(part_ref[core, 1, s], sib[1, s])
            return carry

        lax.fori_loop(0, z + 1, pair_one, 0)

        def z_start(s, carry):
            @pl.when(z + s >= RING)
            def _():
                z_copy(s).start()
            return carry

        lax.fori_loop(1, RING, z_start, 0)

    @pl.when(plane == 0)
    def _():
        def fold(s, carry):
            spot = (z + s) % RING
            x_copy(s).wait_recv()
            pair[0, spot] = add(pair[0, spot], xbuf[spot])

            @pl.when(s > 0)
            def _():
                z_copy(s).start()
            return carry

        lax.fori_loop(0, RING, fold, 0)

    kg_ref[...] = pair[plane, z].astype(jnp.float32)[None]

    def z_land(s, carry):
        @pl.when((plane == 0) | (z + s < RING))
        def _():
            source = (z + s) % RING
            z_arrived(source)
            kg_ref[...] += zbuf[source].astype(jnp.float32)[None]
        return carry

    lax.fori_loop(1, RING, z_land, 0)
    vg_ref[...] = kg_ref[...].astype(jnp.bfloat16)

    def g_land(s, carry):
        g_copy(s).wait_recv()
        return carry

    lax.fori_loop(1, groups, g_land, 0)
    for t in range(slots):
        moved_ref[t] = landed[plan_ref[0, t]]

    def g_left(s, carry):
        g_copy(s).wait_send()
        return carry

    lax.fori_loop(1, groups, g_left, 0)
    s_copy(0).wait_send()

    @pl.when(plane == 1)
    def _():
        s_copy(1).wait_send()

        def x_left(s, carry):
            x_copy(s).wait_send()
            return carry

        lax.fori_loop(0, RING, x_left, 0)

    def z_left(s, carry):
        @pl.when((plane == 0) | (z + s >= RING))
        def _():
            z_copy(s).wait_send()
        return carry

    lax.fori_loop(1, RING, z_left, 0)


NT = (((1,), (1,)), ((), ()))
TN = (((0,), (0,)), ((), ()))
NN = (((1,), (0,)), ((), ()))


def dot(a, b, dims):
    return lax.dot_general(a, b, dims, preferred_element_type=jnp.float32)


def attend_kernel(heads, tile, where_ref, q_ref, g_ref, kv_ref, starts_ref,
                  attn_ref, dq_ref, part_ref,
                  qh, gh, qs, gs, scores, probs, top, total, outT, dqT, dotT):
    tok = q_ref.shape[0]
    rows = heads * tok
    wide = 2 * tok
    scale = 1.0 / math.sqrt(HDIM)
    to_two = scale / math.log(2.0)
    ctx = where_ref[0]
    first = where_ref[1] // tile
    last = ctx * tok // tile
    chunks = [slice(n * wide, (n + 1) * wide) for n in range(rows // wide)]

    for h in range(heads):
        part = slice(h * tok, (h + 1) * tok)
        qh[part] = q_ref[:, h * HDIM:(h + 1) * HDIM]
        gh[part] = g_ref[:, h * HDIM:(h + 1) * HDIM]
    part_ref[...] = jnp.zeros_like(part_ref)
    top[...] = jnp.full_like(top, MASKED)
    total[...] = jnp.zeros_like(total)
    outT[...] = jnp.zeros_like(outT)
    dqT[...] = jnp.zeros_like(dqT)

    def fold(x):
        return x.reshape(tile // 8, 8, x.shape[1])

    def rows_of(n):
        return pl.ds(pl.multiple_of(n * tile, tile), tile)

    def score_tile(n, carry):
        keys = kv_ref[rows_of(n), :HDIM]

        def put(bias):
            for c in chunks:
                s = dot(keys, qh[c], NT)
                if bias is not None:
                    s = s + bias
                scores[n, :, c] = s
                top[:, c] = jnp.maximum(top[:, c], jnp.max(fold(s), axis=0))

        masked = (n * tile < where_ref[2]) | (n == last)

        @pl.when(masked)
        def _():
            at = n * tile + lax.broadcasted_iota(jnp.int32, (tile, tok), 0)
            mine = ctx * tok + lax.broadcasted_iota(jnp.int32, (tile, tok), 1)
            bias = jnp.where((at >= starts_ref[...]) & (at <= mine), 0.0, MASKED)
            put(jnp.concatenate([bias, bias], axis=1))

        @pl.when(jnp.logical_not(masked))
        def _():
            put(None)

        return carry

    lax.fori_loop(first, last + 1, score_tile, 0)
    top[...] = jnp.broadcast_to(jnp.max(top[...], axis=0, keepdims=True) * to_two, top.shape)

    def weigh_tile(n, carry):
        values = kv_ref[rows_of(n), HDIM:]
        for c in chunks:
            p = jnp.exp2(scores[n, :, c] * to_two - top[0:1, c])
            total[:, c] += jnp.sum(fold(p), axis=0)
            p = p.astype(jnp.bfloat16)
            probs[n, :, c] = p
            outT[:, c] += dot(values, p, TN)
        return carry

    lax.fori_loop(first, last + 1, weigh_tile, 0)
    inverse = 1.0 / jnp.sum(total[...], axis=0, keepdims=True)
    total[...] = jnp.broadcast_to(inverse, total.shape)

    ones = jnp.ones((8, HDIM), jnp.bfloat16)
    for h in range(heads):
        part = slice(h * tok, (h + 1) * tok)
        cols = slice(h * HDIM, (h + 1) * HDIM)
        out = (outT[:, part] * total[0:1, part]).T.astype(jnp.bfloat16)
        attn_ref[:, cols] = out
        grad = gh[part].astype(jnp.float32)
        prod = grad * out.astype(jnp.float32)
        high = prod.astype(jnp.bfloat16)
        low = (prod - high.astype(jnp.float32)).astype(jnp.bfloat16)
        dotT[:, part] = dot(ones, high, NT) + dot(ones, low, NT)
        back = jnp.broadcast_to(total[0:1, part], (tok, tok)).T
        gs[part] = (grad * back).astype(jnp.bfloat16)
        qs[part] = (qh[part].astype(jnp.float32) * (back * scale)).astype(jnp.bfloat16)

    def back_tile(n, carry):
        keys = kv_ref[rows_of(n), :HDIM]
        values = kv_ref[rows_of(n), HDIM:]
        dk = jnp.zeros((tile, HDIM), jnp.float32)
        dv = jnp.zeros((tile, HDIM), jnp.float32)
        for c in chunks:
            dp = dot(values, gh[c], NT)
            p = probs[n, :, c]
            ds = (p.astype(jnp.float32) * (dp - dotT[0:1, c])).astype(jnp.bfloat16)
            dqT[:, c] += dot(keys, ds, TN)
            dk += dot(ds, qs[c], NN)
            dv += dot(p, gs[c], NN)
        dk = dk.astype(jnp.bfloat16)
        dv = dv.astype(jnp.bfloat16)
        for core in range(CORES):
            here = slice(core * tok, (core + 1) * tok)
            part_ref[core, n, :, :HDIM] = dk[here]
            part_ref[core, n, :, HDIM:] = dv[here]
        return carry

    lax.fori_loop(first, last + 1, back_tile, 0)
    for h in range(heads):
        part = slice(h * tok, (h + 1) * tok)
        cols = slice(h * HDIM, (h + 1) * HDIM)
        dq_ref[:, cols] = (dqT[:, part] * (total[0:1, part] * scale)).T.astype(jnp.bfloat16)


def attend(where, queries, grads, kv, starts, interpret=False):
    tok, width = queries.shape
    heads = width // HDIM
    rows = heads * tok
    tile = CORES * tok
    tiles = kv.shape[0] // tile
    vmem = pl.BlockSpec(memory_space=pltpu.VMEM)
    bf, f32 = jnp.bfloat16, jnp.float32
    return pl.pallas_call(
        functools.partial(attend_kernel, heads, tile),
        out_shape=(
            jax.ShapeDtypeStruct((tok, width), bf),
            jax.ShapeDtypeStruct((tok, width), bf),
            jax.ShapeDtypeStruct((CORES, tiles, tok, 2 * HDIM), bf),
        ),
        in_specs=[pl.BlockSpec(memory_space=pltpu.SMEM)] + [vmem] * 4,
        out_specs=(vmem,) * 3,
        scratch_shapes=[
            pltpu.VMEM((rows, HDIM), bf),
            pltpu.VMEM((rows, HDIM), bf),
            pltpu.VMEM((rows, HDIM), bf),
            pltpu.VMEM((rows, HDIM), bf),
            pltpu.VMEM((tiles, tile, rows), f32),
            pltpu.VMEM((tiles, tile, rows), bf),
            pltpu.VMEM((8, rows), f32),
            pltpu.VMEM((8, rows), f32),
            pltpu.VMEM((HDIM, rows), f32),
            pltpu.VMEM((HDIM, rows), f32),
            pltpu.VMEM((8, rows), f32),
        ],
        compiler_params=pltpu.CompilerParams(vmem_limit_bytes=VMEM_LIMIT),
        interpret=interpret,
    )(where, queries, grads, kv, starts)


def per_device(queries, key_states, value_states, doc_start, move_plan, out_grad):
    tok, width = queries.shape[1:]
    groups = lax.axis_size("dp")
    pieces = lax.axis_size("ctx")
    slots = move_plan.shape[1]
    rows = tok // slots
    ctx = lax.axis_index("ctx")
    vmem = pl.BlockSpec(memory_space=pltpu.VMEM)
    smem = pl.BlockSpec(memory_space=pltpu.SMEM)
    bf, f32 = jnp.bfloat16, jnp.float32
    dma = pltpu.SemaphoreType.DMA

    kv, home = pl.pallas_call(
        functools.partial(gather_kernel, groups, slots),
        out_shape=(
            jax.ShapeDtypeStruct((pieces, tok, 2 * HDIM), bf),
            jax.ShapeDtypeStruct((slots, rows, width), bf),
        ),
        in_specs=[vmem, vmem, vmem, smem],
        out_specs=(vmem, vmem),
        scratch_shapes=[
            pltpu.VMEM((groups, rows, width), bf),
            pltpu.VMEM((groups, rows, width), bf),
            dma((RING,)), dma((RING,)), dma((2 * RING,)), dma((pieces,)),
            dma((groups,)), dma((groups,)),
        ],
        compiler_params=pltpu.CompilerParams(
            collective_id=0, has_side_effects=True, vmem_limit_bytes=VMEM_LIMIT),
    )(key_states, value_states, out_grad.reshape(slots, rows, width), move_plan)

    where = jnp.stack([ctx, doc_start[0, 0], doc_start[0, tok - 1]]).astype(jnp.int32)
    attn, dq, parts = attend(
        where, queries[0], home.reshape(tok, width), kv.reshape(pieces * tok, 2 * HDIM), doc_start)

    moved, _, pair_grad = pl.pallas_call(
        functools.partial(scatter_kernel, groups, slots),
        out_shape=(
            jax.ShapeDtypeStruct((slots, rows, width), bf),
            jax.ShapeDtypeStruct((1, tok, 2 * HDIM), f32),
            jax.ShapeDtypeStruct((1, tok, 2 * HDIM), bf),
        ),
        in_specs=[vmem, vmem, smem],
        out_specs=(vmem, vmem, vmem),
        scratch_shapes=[
            pltpu.VMEM((groups, rows, width), bf),
            pltpu.VMEM((groups, rows, width), bf),
            pltpu.VMEM((2, RING, tok, 2 * HDIM), bf),
            pltpu.VMEM((2, RING, tok, 2 * HDIM), bf),
            pltpu.VMEM((RING, tok, 2 * HDIM), bf),
            pltpu.VMEM((RING, tok, 2 * HDIM), bf),
            dma((2,)), dma((2,)), dma((RING,)), dma((RING,)), dma((RING,)), dma((RING,)),
            dma((groups,)), dma((groups,)),
        ],
        compiler_params=pltpu.CompilerParams(
            collective_id=1, has_side_effects=True, vmem_limit_bytes=VMEM_LIMIT),
    )(attn.reshape(slots, rows, width), parts.reshape(CORES, 2, RING, tok, 2 * HDIM), move_plan)
    return (
        moved.reshape(1, tok, width),
        dq[None],
        pair_grad[:, :, :HDIM],
        pair_grad[:, :, HDIM:],
    )


def solution(mesh):
    split = P("dp", "ctx", None)
    return jax.shard_map(
        per_device,
        mesh=mesh,
        in_specs=(split, split, split, P("dp", "ctx"), P("ctx", None), split),
        out_specs=(split, split, split, split),
        check_vma=False,
    )
```

```python
import functools
import math

import jax
import jax.numpy as jnp
from jax import lax
from jax.experimental import pallas as pl
from jax.experimental.pallas import tpu as pltpu
from jax.sharding import PartitionSpec as P

HDIM = 128
MASKED = -1e30
MESH = pl.DeviceIdType.MESH
VMEM_LIMIT = 58 * 1024 * 1024
CORES = 2
RING = 8
PAIRS = 8
NT = (((1,), (1,)), ((), ()))
TN = (((0,), (0,)), ((), ()))
NN = (((1,), (0,)), ((), ()))


def dot(a, b, dims):
    return lax.dot_general(a, b, dims, preferred_element_type=jnp.float32)


def add(a, b):
    return (a.astype(jnp.float32) + b.astype(jnp.float32)).astype(jnp.bfloat16)


def ctx_of(plane, z, core):
    return (plane * RING + z) * CORES + core


def remote(src, dst, send_sem, recv_sem, **axes):
    return pltpu.make_async_remote_copy(
        src_ref=src, dst_ref=dst, send_sem=send_sem, recv_sem=recv_sem,
        device_id=axes, device_id_type=MESH,
    )


def loop(low, high, step):
    def body(i, carry):
        step(i)
        return carry

    lax.fori_loop(low, high, body, 0)


def slot_of(plan_ref, s, slots):
    found = jnp.int32(0)
    for t in range(slots):
        found = jnp.where(plan_ref[0, t] == s, jnp.int32(t), found)
    return found


def kernel(groups, slots, heads,
           q_ref, k_ref, v_ref, starts_ref, plan_ref, grad_ref,
           moved_ref, dq_ref, kg_ref, vg_ref,
           kv, qh, gh, qs, gs, scores, probs, top, total, outT, dqT, dotT, attn,
           stage_g, landed_g, stage_o, landed_o, part, sib, pair, xbuf, zbuf, acc,
           send_f, send_x, send_s, recv_kv, send_g, recv_g, send_o, recv_o,
           send_s2, recv_s2, send_x2, recv_x2, send_z2, recv_z2):
    tok = q_ref.shape[0]
    block_rows = tok // slots
    rows = heads * tok
    tile = CORES * tok
    scale = 1.0 / math.sqrt(HDIM)
    to_two = scale / math.log(2.0)
    group = lax.axis_index("dp")
    ctx = lax.axis_index("ctx")
    chip = ctx // CORES
    plane, z, core = chip // RING, chip % RING, ctx % CORES
    own_pair = chip // 2
    wide = rows // 2
    chunks = [slice(n * wide, (n + 1) * wide) for n in range(2)]

    barrier = pltpu.get_barrier_semaphore()

    def hello(**axes):
        pl.semaphore_signal(barrier, inc=1, device_id=axes, device_id_type=MESH)

    loop(1, groups, lambda s: hello(dp=(group + s) % groups))
    loop(1, RING, lambda s: hello(ctx=ctx_of(plane, (z + s) % RING, core)))
    hello(ctx=ctx_of(1 - plane, z, core))
    hello(ctx=ctx_of(plane, z, 1 - core))

    kv[ctx, :, :HDIM] = k_ref[0]
    kv[ctx, :, HDIM:] = v_ref[0]
    for s in range(groups):
        block = grad_ref[slot_of(plan_ref, s, slots)]
        if s == 0:
            landed_g[0] = block
        else:
            stage_g[s] = block
    for h in range(heads):
        qh[h * tok:(h + 1) * tok] = q_ref[:, h * HDIM:(h + 1) * HDIM]
    top[...] = jnp.full_like(top, MASKED)
    total[...] = jnp.zeros_like(total)
    outT[...] = jnp.zeros_like(outT)
    dqT[...] = jnp.zeros_like(dqT)
    pl.semaphore_wait(barrier, groups - 1 + RING - 1 + 2)

    def origin(i):
        hop = (i + 1) // 2
        return (z + jnp.where(i % 2 == 1, RING - hop, hop)) % RING

    def ring_copy(block, sem, ahead):
        return remote(kv.at[block], kv.at[block], send_f.at[sem], recv_kv.at[block],
                      ctx=ctx_of(plane, (z + jnp.where(ahead, 1, RING - 1)) % RING, core))

    def f_copy(i):
        return ring_copy(ctx_of(plane, origin(i), core), i, i % 2 == 1)

    def x_copy(i):
        block = ctx_of(0, origin(i), core)
        return remote(kv.at[block], kv.at[block], send_x.at[i], recv_kv.at[block],
                      ctx=ctx_of(1, z, core))

    def s_copy(owner, i):
        block = ctx_of(owner, origin(i), core)
        return remote(kv.at[block], kv.at[block], send_s.at[owner * RING + i],
                      recv_kv.at[block], ctx=ctx_of(plane, z, 1 - core))

    def g_copy(s):
        return remote(stage_g.at[s], landed_g.at[s], send_g.at[s], recv_g.at[s],
                      dp=(group + groups - s) % groups)

    def o_copy(s):
        return remote(stage_o.at[s], landed_o.at[s], send_o.at[s], recv_o.at[s],
                      dp=(group + s) % groups)

    def arrived(block):
        remote(kv.at[block], kv.at[block], send_f.at[0], recv_kv.at[block],
               ctx=ctx_of(plane, z, 1 - core)).wait_recv()

    ring_copy(ctx, 0, True).start()
    ring_copy(ctx, 6, False).start()

    @pl.when(plane == 0)
    def _():
        x_copy(0).start()

    s_copy(plane, 0).start()
    loop(1, groups, lambda s: g_copy(s).start())

    def fold(x):
        return x.reshape(x.shape[0] // 8, 8, x.shape[1])

    def score(n):
        keys = kv[pl.ds(CORES * n, CORES), :, :HDIM].reshape(tile, HDIM)
        at = n * tile + lax.broadcasted_iota(jnp.int32, (tile, tok), 0)
        mine = ctx * tok + lax.broadcasted_iota(jnp.int32, (tile, tok), 1)
        bias = jnp.where((at >= starts_ref[...]) & (at <= mine), 0.0, MASKED)
        bias = jnp.concatenate([bias] * (wide // tok), axis=1)
        for c in chunks:
            s = dot(keys, qh[c], NT) + bias
            scores[n, :, c] = s
            top[:, c] = jnp.maximum(top[:, c], jnp.max(fold(s), axis=0))

    def gather_step(i):
        @pl.when((i >= 1) & (i < RING))
        def _():
            arrived(ctx_of(plane, origin(i), core))

            @pl.when(i < RING - 2)
            def _():
                f_copy(i).start()

            @pl.when(plane == 0)
            def _():
                x_copy(i).start()

            s_copy(plane, i).start()

        @pl.when((plane == 1) & (i >= 1) & (i <= RING))
        def _():
            arrived(ctx_of(0, origin(i - 1), core))
            s_copy(0, i - 1).start()

        @pl.when((i >= 1) & (i <= RING))
        def _():
            near = plane * RING + origin(i - 1)
            arrived(CORES * near + 1 - core)

            @pl.when(near <= 2 * own_pair + 1)
            def _():
                score(near)

        @pl.when((plane == 1) & (i >= 2))
        def _():
            arrived(CORES * origin(i - 2) + 1 - core)
            score(origin(i - 2))

    loop(0, RING + 2, gather_step)
    top[...] = jnp.broadcast_to(jnp.max(top[...], axis=0, keepdims=True) * to_two, top.shape)

    def weigh(u):
        values = kv[pl.ds(2 * CORES * u, 2 * CORES), :, HDIM:].reshape(2 * tile, HDIM)
        for c in chunks:
            s = scores[pl.ds(2 * u, 2), :, c].reshape(2 * tile, wide)
            p = jnp.exp2(s * to_two - top[0:1, c])
            total[:, c] += jnp.sum(fold(p), axis=0)
            p = p.astype(jnp.bfloat16)
            probs[u, :, c] = p
            outT[:, c] += dot(values, p, TN)

    loop(0, own_pair + 1, weigh)
    inverse = 1.0 / jnp.sum(total[...], axis=0, keepdims=True)
    total[...] = jnp.broadcast_to(inverse, total.shape)
    for h in range(heads):
        mine = slice(h * tok, (h + 1) * tok)
        out = (outT[:, mine] * total[0:1, mine]).T.astype(jnp.bfloat16)
        attn[:, :, h * HDIM:(h + 1) * HDIM] = out.reshape(slots, block_rows, HDIM)
    for s in range(groups):
        block = attn[slot_of(plan_ref, s, slots)]
        if s == 0:
            landed_o[0] = block
        else:
            stage_o[s] = block
    loop(1, groups, lambda s: o_copy(s).start())

    loop(1, groups, lambda s: g_copy(s).wait_recv())
    for t in range(slots):
        block = landed_g[plan_ref[0, t]]
        for h in range(heads):
            first = h * tok + t * block_rows
            gh[first:first + block_rows] = block[:, h * HDIM:(h + 1) * HDIM]
    ones = jnp.ones((8, HDIM), jnp.bfloat16)
    for h in range(heads):
        mine = slice(h * tok, (h + 1) * tok)
        out = attn[:, :, h * HDIM:(h + 1) * HDIM].reshape(tok, HDIM)
        grad = gh[mine].astype(jnp.float32)
        prod = grad * out.astype(jnp.float32)
        high = prod.astype(jnp.bfloat16)
        low = (prod - high.astype(jnp.float32)).astype(jnp.bfloat16)
        dotT[:, mine] = dot(ones, high, NT) + dot(ones, low, NT)
        back = jnp.broadcast_to(total[0:1, mine], (tok, tok)).T
        gs[mine] = (grad * back).astype(jnp.bfloat16)
        qs[mine] = (qh[mine].astype(jnp.float32) * (back * scale)).astype(jnp.bfloat16)

    far = plane * (PAIRS // 2)

    def pair_at(i):
        return jnp.where(i < far, (z // 2 + 1 + i) % (PAIRS // 2), far + z // 2 - (i - far))

    def s2_copy(u):
        return remote(part.at[u, 1 - core], sib.at[u], send_s2.at[u], recv_s2.at[u],
                      ctx=ctx_of(plane, z, 1 - core))

    def x2_copy(u):
        return remote(pair.at[u], xbuf.at[u], send_x2.at[u], recv_x2.at[u],
                      ctx=ctx_of(1 - plane, z, core))

    def z2_copy(spot):
        return remote(pair.at[far + spot // 2, spot % 2], zbuf.at[z], send_z2.at[spot],
                      recv_z2.at[z], ctx=ctx_of(plane, spot, core))

    def back(u):
        keys = kv[pl.ds(2 * CORES * u, 2 * CORES), :, :HDIM].reshape(2 * tile, HDIM)
        values = kv[pl.ds(2 * CORES * u, 2 * CORES), :, HDIM:].reshape(2 * tile, HDIM)
        dp = dot(values, gh[...], NT)
        p = probs[u]
        ds = (p.astype(jnp.float32) * (dp - dotT[0:1])).astype(jnp.bfloat16)
        dqT[...] += dot(keys, ds, TN)
        dk = dot(ds, qs[...], NN).astype(jnp.bfloat16)
        dv = dot(p, gs[...], NN).astype(jnp.bfloat16)
        for which in range(2):
            for c in range(CORES):
                first = (which * CORES + c) * tok
                part[u, c, which, :, :HDIM] = dk[first:first + tok]
                part[u, c, which, :, HDIM:] = dv[first:first + tok]

    def pass_on(u):
        s2_copy(u).wait_recv()
        pair[u] = add(part[u, core], sib[u])

        @pl.when(u < far)
        def _():
            x2_copy(u).start()

        @pl.when((plane == 1) & (u >= far))
        def _():
            for which in range(2):
                spot = (u - far) * 2 + which

                @pl.when(spot < z)
                def _():
                    z2_copy(spot).start()

    def back_step(i):
        u = pair_at(i)
        back(u)
        s2_copy(u).start()

        @pl.when(i >= 1)
        def _():
            pass_on(pair_at(i - 1))

    loop(0, own_pair + 1, back_step)
    pass_on(pair_at(own_pair))

    for h in range(heads):
        mine = slice(h * tok, (h + 1) * tok)
        dq_ref[:, h * HDIM:(h + 1) * HDIM] = (
            dqT[:, mine] * (total[0:1, mine] * scale)).T.astype(jnp.bfloat16)

    @pl.when(plane == 0)
    def _():
        def fold_in(j):
            u = (z // 2 + 1 + j) % (PAIRS // 2)
            x2_copy(u).wait_recv()

            @pl.when(u <= own_pair)
            def _():
                pair[u] = add(pair[u], xbuf[u])

            @pl.when(u > own_pair)
            def _():
                pair[u] = xbuf[u]

            for which in range(2):
                spot = u * 2 + which

                @pl.when(spot != z)
                def _():
                    z2_copy(spot).start()

        loop(0, PAIRS // 2, fold_in)

    acc[...] = pair[own_pair, z % 2].astype(jnp.float32)

    def z_land(s):
        source = (z + s) % RING

        @pl.when((plane == 0) | (source > z))
        def _():
            remote(zbuf.at[source], zbuf.at[source], send_z2.at[0], recv_z2.at[source],
                   ctx=ctx_of(plane, source, core)).wait_recv()
            acc[...] += zbuf[source].astype(jnp.float32)

    loop(1, RING, z_land)
    kg_ref[0] = acc[:, :HDIM].astype(jnp.bfloat16)
    vg_ref[0] = acc[:, HDIM:].astype(jnp.bfloat16)

    loop(1, groups, lambda s: o_copy(s).wait_recv())
    for t in range(slots):
        moved_ref[t] = landed_o[plan_ref[0, t]]

    def exchanged(s):
        g_copy(s).wait_send()
        o_copy(s).wait_send()

    loop(1, groups, exchanged)
    ring_copy(ctx, 0, True).wait_send()
    ring_copy(ctx, 6, False).wait_send()
    loop(1, RING - 2, lambda i: f_copy(i).wait_send())

    def gathered(i):
        s_copy(plane, i).wait_send()

        @pl.when(plane == 0)
        def _():
            x_copy(i).wait_send()

        @pl.when(plane == 1)
        def _():
            s_copy(0, i).wait_send()

        @pl.when((i < z) | ((plane == 0) & (i != z)))
        def _():
            z2_copy(i).wait_send()

        @pl.when(i < far)
        def _():
            x2_copy(i).wait_send()

    loop(0, RING, gathered)
    loop(0, own_pair + 1, lambda i: s2_copy(pair_at(i)).wait_send())


def per_device(queries, key_states, value_states, doc_start, move_plan, out_grad):
    tok, width = queries.shape[1:]
    heads = width // HDIM
    rows = heads * tok
    groups = lax.axis_size("dp")
    pieces = lax.axis_size("ctx")
    slots = move_plan.shape[1]
    block_rows = tok // slots
    tile = CORES * tok
    vmem = pl.BlockSpec(memory_space=pltpu.VMEM)
    smem = pl.BlockSpec(memory_space=pltpu.SMEM)
    bf, f32 = jnp.bfloat16, jnp.float32
    dma = pltpu.SemaphoreType.DMA
    blocks = pltpu.VMEM((groups, block_rows, width), bf)
    heads_bf = pltpu.VMEM((rows, HDIM), bf)

    moved, dq, kg, vg = pl.pallas_call(
        functools.partial(kernel, groups, slots, heads),
        out_shape=(
            jax.ShapeDtypeStruct((slots, block_rows, width), bf),
            jax.ShapeDtypeStruct((tok, width), bf),
            jax.ShapeDtypeStruct((1, tok, HDIM), bf),
            jax.ShapeDtypeStruct((1, tok, HDIM), bf),
        ),
        in_specs=[vmem, vmem, vmem, vmem, smem, vmem],
        out_specs=(vmem,) * 4,
        scratch_shapes=[
            pltpu.VMEM((pieces, tok, 2 * HDIM), bf),
            heads_bf, heads_bf, heads_bf, heads_bf,
            pltpu.VMEM((2 * PAIRS, tile, rows), f32),
            pltpu.VMEM((PAIRS, 2 * tile, rows), bf),
            pltpu.VMEM((8, rows), f32),
            pltpu.VMEM((8, rows), f32),
            pltpu.VMEM((HDIM, rows), f32),
            pltpu.VMEM((HDIM, rows), f32),
            pltpu.VMEM((8, rows), f32),
            pltpu.VMEM((slots, block_rows, width), bf),
            blocks, blocks, blocks, blocks,
            pltpu.VMEM((PAIRS, CORES, 2, tok, 2 * HDIM), bf),
            pltpu.VMEM((PAIRS, 2, tok, 2 * HDIM), bf),
            pltpu.VMEM((PAIRS, 2, tok, 2 * HDIM), bf),
            pltpu.VMEM((PAIRS // 2, 2, tok, 2 * HDIM), bf),
            pltpu.VMEM((RING, tok, 2 * HDIM), bf),
            pltpu.VMEM((tok, 2 * HDIM), f32),
            dma((RING,)), dma((RING,)), dma((2 * RING,)), dma((pieces,)),
            dma((groups,)), dma((groups,)), dma((groups,)), dma((groups,)),
            dma((PAIRS,)), dma((PAIRS,)), dma((PAIRS // 2,)), dma((PAIRS // 2,)),
            dma((RING,)), dma((RING,)),
        ],
        compiler_params=pltpu.CompilerParams(
            collective_id=0, has_side_effects=True, vmem_limit_bytes=VMEM_LIMIT),
    )(
        queries[0], key_states, value_states, doc_start, move_plan,
        out_grad.reshape(slots, block_rows, width),
    )
    return moved.reshape(1, tok, width), dq[None], kg, vg


def solution(mesh):
    split = P("dp", "ctx", None)
    return jax.shard_map(
        per_device,
        mesh=mesh,
        in_specs=(split, split, split, P("dp", "ctx"), P("ctx", None), split),
        out_specs=(split, split, split, split),
        check_vma=False,
    )
```

```python
import functools
import math

import jax
import jax.numpy as jnp
from jax import lax
from jax.experimental import pallas as pl
from jax.experimental.pallas import tpu as pltpu
from jax.sharding import PartitionSpec as P

HDIM = 128
MASKED = -1e30
MESH = pl.DeviceIdType.MESH
VMEM_LIMIT = 58 * 1024 * 1024
CORES = 2
RING = 8
PAIRS = 8
NT = (((1,), (1,)), ((), ()))
TN = (((0,), (0,)), ((), ()))
NN = (((1,), (0,)), ((), ()))


def dot(a, b, dims):
    return lax.dot_general(a, b, dims, preferred_element_type=jnp.float32)


def add(a, b):
    return (a.astype(jnp.float32) + b.astype(jnp.float32)).astype(jnp.bfloat16)


def ctx_of(plane, z, core):
    return (plane * RING + z) * CORES + core


def remote(src, dst, send_sem, recv_sem, **axes):
    return pltpu.make_async_remote_copy(
        src_ref=src, dst_ref=dst, send_sem=send_sem, recv_sem=recv_sem,
        device_id=axes, device_id_type=MESH,
    )


def loop(low, high, step):
    def body(i, carry):
        step(i)
        return carry

    lax.fori_loop(low, high, body, 0)


def slot_of(plan_ref, s, slots):
    found = jnp.int32(0)
    for t in range(slots):
        found = jnp.where(plan_ref[0, t] == s, jnp.int32(t), found)
    return found


def kernel(groups, slots, heads,
           q_ref, k_ref, v_ref, starts_ref, plan_ref, grad_ref,
           moved_ref, dq_ref, kg_ref, vg_ref,
           keys_all, values_all, eye, qh, gh, qs, gs, scores, probs, top, total, outT, dqT, dotT, attn,
           stage_g, landed_g, stage_o, landed_o, part, sib, pair, xbuf, zbuf, acc,
           send_f, send_x, send_s, recv_kv, send_g, recv_g, send_o, recv_o,
           send_s2, recv_s2, send_x2, recv_x2, send_z2, recv_z2):
    tok = q_ref.shape[0]
    block_rows = tok // slots
    rows = heads * tok
    tile = CORES * tok
    scale = 1.0 / math.sqrt(HDIM)
    to_two = scale / math.log(2.0)
    group = lax.axis_index("dp")
    ctx = lax.axis_index("ctx")
    chip = ctx // CORES
    plane, z, core = chip // RING, chip % RING, ctx % CORES
    own_pair = chip // 2
    wide = rows // 2
    chunks = [slice(n * wide, (n + 1) * wide) for n in range(2)]

    def flip(x):
        return dot(eye[...], x, NT)

    barrier = pltpu.get_barrier_semaphore()

    def hello(**axes):
        pl.semaphore_signal(barrier, inc=1, device_id=axes, device_id_type=MESH)

    loop(1, groups, lambda s: hello(dp=(group + s) % groups))
    loop(1, RING, lambda s: hello(ctx=ctx_of(plane, (z + s) % RING, core)))
    hello(ctx=ctx_of(1 - plane, z, core))
    hello(ctx=ctx_of(plane, z, 1 - core))

    keys_all[ctx] = k_ref[0]
    values_all[ctx] = v_ref[0]
    for s in range(groups):
        block = grad_ref[slot_of(plan_ref, s, slots)]
        if s == 0:
            landed_g[0] = block
        else:
            stage_g[s] = block
    for h in range(heads):
        qh[h * tok:(h + 1) * tok] = q_ref[:, h * HDIM:(h + 1) * HDIM]
    eye[...] = jnp.where(
        lax.broadcasted_iota(jnp.int32, (tok, tok), 0)
        == lax.broadcasted_iota(jnp.int32, (tok, tok), 1), 1.0, 0.0).astype(jnp.bfloat16)
    top[...] = jnp.full_like(top, MASKED)
    total[...] = jnp.zeros_like(total)
    outT[...] = jnp.zeros_like(outT)
    dqT[...] = jnp.zeros_like(dqT)
    pl.semaphore_wait(barrier, groups - 1 + RING - 1 + 2)

    def offset(i):
        return jnp.where(i == 0, 0, jnp.where(i % 2 == 1, RING // 2 + i // 2, RING // 2 - i // 2))

    def origin(i):
        return (z + RING - offset(i)) % RING

    def goes(i):
        return (plane == 0) | ((z + offset(i)) % RING >= z // 2 * 2)

    def comes(i):
        return (plane == 0) | (origin(i) <= z // 2 * 2 + 1)

    def around(i):
        hop = (i + 1) // 2
        return (z + jnp.where(i % 2 == 1, RING - hop, hop)) % RING

    def stream(kind):
        return (keys_all, 0) if kind == 0 else (values_all, 1)

    def source(kind, i):
        return origin(i) if kind == 0 else around(i)

    def f_copy(i):
        return remote(keys_all.at[ctx], keys_all.at[ctx], send_f.at[0, i], recv_kv.at[0, ctx],
                      ctx=ctx_of(plane, (z + offset(i)) % RING, core))

    def ring_copy(kind, i, sem, ahead):
        block = ctx_of(0 if kind == 2 else plane, around(i), core)
        return remote(values_all.at[block], values_all.at[block], send_f.at[kind, sem],
                      recv_kv.at[1, block],
                      ctx=ctx_of(plane, (z + jnp.where(ahead, 1, RING - 1)) % RING, core))

    def r_copy(kind, i):
        return ring_copy(kind, i, i, i % 2 == 1)

    def first_copy(kind, ahead):
        return ring_copy(kind, 0, 0 if ahead else RING - 1, ahead)

    def x_copy(kind, i):
        buf, which = stream(kind)
        block = ctx_of(0, source(kind, i), core)
        return remote(buf.at[block], buf.at[block], send_x.at[which, i], recv_kv.at[which, block],
                      ctx=ctx_of(1, z, core))

    def s_copy(kind, owner, i):
        buf, which = stream(kind)
        block = ctx_of(owner, source(kind, i), core)
        return remote(buf.at[block], buf.at[block], send_s.at[which, owner * RING + i],
                      recv_kv.at[which, block], ctx=ctx_of(plane, z, 1 - core))

    def g_copy(s):
        return remote(stage_g.at[s], landed_g.at[s], send_g.at[s], recv_g.at[s],
                      dp=(group + groups - s) % groups)

    def o_copy(s):
        return remote(stage_o.at[s], landed_o.at[s], send_o.at[s], recv_o.at[s],
                      dp=(group + s) % groups)

    def arrived(kind, block):
        buf, which = stream(kind)
        remote(buf.at[block], buf.at[block], send_f.at[0, 0], recv_kv.at[which, block],
               ctx=ctx_of(plane, z, 1 - core)).wait_recv()

    for kind in range(2):
        s_copy(kind, plane, 0).start()

        @pl.when(plane == 0)
        def _():
            x_copy(kind, 0).start()

    def spread_out(i):
        @pl.when(goes(i))
        def _():
            f_copy(i).start()

    loop(1, RING, spread_out)
    first_copy(1, True).start()
    first_copy(1, False).start()
    loop(1, groups, lambda s: g_copy(s).start())

    def fold(x):
        return x.reshape(x.shape[0] // 8, 8, x.shape[1])

    def score(n):
        keys = keys_all[pl.ds(CORES * n, CORES)].reshape(tile, HDIM)
        at = n * tile + lax.broadcasted_iota(jnp.int32, (tile, tok), 0)
        mine = ctx * tok + lax.broadcasted_iota(jnp.int32, (tile, tok), 1)
        bias = jnp.where((at >= starts_ref[...]) & (at <= mine), 0.0, MASKED)
        bias = jnp.concatenate([bias] * (wide // tok), axis=1)
        for c in chunks:
            s = dot(keys, qh[c], NT) + bias
            scores[n, :, c] = s
            top[:, c] = jnp.maximum(top[:, c], jnp.max(fold(s), axis=0))

    def gather_step(i):
        @pl.when((i >= 1) & (i < RING))
        def _():
            @pl.when(comes(i))
            def _():
                arrived(0, ctx_of(plane, origin(i), core))

                @pl.when(plane == 0)
                def _():
                    x_copy(0, i).start()

                s_copy(0, plane, i).start()

            arrived(1, ctx_of(plane, around(i), core))

            @pl.when(i < RING - 2)
            def _():
                r_copy(1, i).start()

            s_copy(1, plane, i).start()

        @pl.when((plane == 1) & (i >= 1) & (i <= RING))
        def _():
            j = i - 1
            arrived(0, ctx_of(0, origin(j), core))
            s_copy(0, 0, j).start()
            arrived(1, ctx_of(0, around(j), core))

            @pl.when(j == 0)
            def _():
                first_copy(2, True).start()
                first_copy(2, False).start()

            @pl.when((j >= 1) & (j < RING - 2))
            def _():
                r_copy(2, j).start()

            s_copy(1, 0, j).start()

        @pl.when((i >= 1) & (i <= RING))
        def _():
            near = plane * RING + origin(i - 1)

            @pl.when(comes(i - 1))
            def _():
                arrived(0, CORES * near + 1 - core)

            @pl.when(near <= 2 * own_pair + 1)
            def _():
                score(near)

        @pl.when((plane == 1) & (i >= 2))
        def _():
            arrived(0, CORES * origin(i - 2) + 1 - core)
            score(origin(i - 2))

    loop(0, RING + 2, gather_step)
    top[...] = jnp.broadcast_to(jnp.max(top[...], axis=0, keepdims=True) * to_two, top.shape)

    loop(0, RING, lambda i: arrived(1, ctx_of(plane, i, 1 - core)))

    @pl.when(plane == 1)
    def _():
        loop(0, RING, lambda i: arrived(1, ctx_of(0, i, 1 - core)))

    def weigh(u):
        values = values_all[pl.ds(2 * CORES * u, 2 * CORES)].reshape(2 * tile, HDIM)
        for c in chunks:
            s = scores[pl.ds(2 * u, 2), :, c].reshape(2 * tile, wide)
            p = jnp.exp2(s * to_two - top[0:1, c])
            total[:, c] += jnp.sum(fold(p), axis=0)
            p = p.astype(jnp.bfloat16)
            probs[u, :, c] = p
            outT[:, c] += dot(values, p, TN)

    loop(0, own_pair + 1, weigh)
    inverse = 1.0 / jnp.sum(total[...], axis=0, keepdims=True)
    total[...] = jnp.broadcast_to(inverse, total.shape)
    for h in range(heads):
        mine = slice(h * tok, (h + 1) * tok)
        out = flip((outT[:, mine] * total[0:1, mine]).astype(jnp.bfloat16)).astype(jnp.bfloat16)
        attn[:, :, h * HDIM:(h + 1) * HDIM] = out.reshape(slots, block_rows, HDIM)
    for s in range(groups):
        block = attn[slot_of(plan_ref, s, slots)]
        if s == 0:
            landed_o[0] = block
        else:
            stage_o[s] = block
    loop(1, groups, lambda s: o_copy(s).start())

    loop(1, groups, lambda s: g_copy(s).wait_recv())
    for t in range(slots):
        block = landed_g[plan_ref[0, t]]
        for h in range(heads):
            first = h * tok + t * block_rows
            gh[first:first + block_rows] = block[:, h * HDIM:(h + 1) * HDIM]
    ones = jnp.ones((8, HDIM), jnp.bfloat16)
    for h in range(heads):
        mine = slice(h * tok, (h + 1) * tok)
        out = attn[:, :, h * HDIM:(h + 1) * HDIM].reshape(tok, HDIM)
        grad = gh[mine].astype(jnp.float32)
        prod = grad * out.astype(jnp.float32)
        high = prod.astype(jnp.bfloat16)
        low = (prod - high.astype(jnp.float32)).astype(jnp.bfloat16)
        dotT[:, mine] = dot(ones, high, NT) + dot(ones, low, NT)
        spread = jnp.broadcast_to(total[0:1, mine], (HDIM, tok))
        coarse = spread.astype(jnp.bfloat16)
        fine = (spread - coarse.astype(jnp.float32)).astype(jnp.bfloat16)
        back = flip(coarse) + flip(fine)
        gs[mine] = (grad * back).astype(jnp.bfloat16)
        qs[mine] = (qh[mine].astype(jnp.float32) * (back * scale)).astype(jnp.bfloat16)

    far = plane * (PAIRS // 2)

    near_pairs = z // 2 + 1

    def far_pair(turn):
        flip_way = (turn == 1) == (z // 2 % 2 == 0)
        step = jnp.where(turn == 0, 2, jnp.where(turn == 3, 0, jnp.where(flip_way, 1, 3)))
        return (z // 2 + step) % (PAIRS // 2)

    def pair_at(i):
        away = (plane == 1) & ((i % 2 == 0) | (i >= 2 * near_pairs))
        turn = jnp.where(i < 2 * near_pairs, i // 2, i - near_pairs)
        near = (2 * near_pairs - 2 - jnp.where(plane == 1, turn, i)) % near_pairs
        return jnp.where(away, far_pair(turn), far + near)

    def s2_copy(u):
        return remote(part.at[u, 1 - core], sib.at[u], send_s2.at[u], recv_s2.at[u],
                      ctx=ctx_of(plane, z, 1 - core))

    def x2_copy(u):
        return remote(pair.at[u], xbuf.at[u], send_x2.at[u], recv_x2.at[u],
                      ctx=ctx_of(1 - plane, z, core))

    def z2_copy(spot):
        return remote(pair.at[far + spot // 2, spot % 2], zbuf.at[z], send_z2.at[spot],
                      recv_z2.at[z], ctx=ctx_of(plane, spot, core))

    def back(u):
        keys = keys_all[pl.ds(2 * CORES * u, 2 * CORES)].reshape(2 * tile, HDIM)
        values = values_all[pl.ds(2 * CORES * u, 2 * CORES)].reshape(2 * tile, HDIM)
        dp = dot(values, gh[...], NT)
        p = probs[u]
        ds = (p.astype(jnp.float32) * (dp - dotT[0:1])).astype(jnp.bfloat16)
        dqT[...] += dot(keys, ds, TN)
        dk = dot(ds, qs[...], NN).astype(jnp.bfloat16)
        dv = dot(p, gs[...], NN).astype(jnp.bfloat16)
        for which in range(2):
            for c in range(CORES):
                first = (which * CORES + c) * tok
                part[u, c, which, :, :HDIM] = dk[first:first + tok]
                part[u, c, which, :, HDIM:] = dv[first:first + tok]

    def pass_on(u):
        s2_copy(u).wait_recv()
        pair[u] = add(part[u, core], sib[u])

        @pl.when(u < far)
        def _():
            x2_copy(u).start()

        @pl.when((plane == 1) & (u >= far))
        def _():
            for which in range(2):
                spot = (u - far) * 2 + which

                @pl.when(spot < z)
                def _():
                    z2_copy(spot).start()

    def back_step(i):
        u = pair_at(i)
        back(u)
        s2_copy(u).start()

        @pl.when(i >= 1)
        def _():
            pass_on(pair_at(i - 1))

    loop(0, own_pair + 1, back_step)
    pass_on(pair_at(own_pair))

    for h in range(heads):
        mine = slice(h * tok, (h + 1) * tok)
        dq_ref[:, h * HDIM:(h + 1) * HDIM] = flip(
            (dqT[:, mine] * (total[0:1, mine] * scale)).astype(jnp.bfloat16)).astype(jnp.bfloat16)

    @pl.when(plane == 0)
    def _():
        def fold_in(j):
            u = far_pair(j)
            x2_copy(u).wait_recv()

            @pl.when(u <= own_pair)
            def _():
                pair[u] = add(pair[u], xbuf[u])

            @pl.when(u > own_pair)
            def _():
                pair[u] = xbuf[u]

            for which in range(2):
                spot = u * 2 + which

                @pl.when(spot != z)
                def _():
                    z2_copy(spot).start()

        loop(0, PAIRS // 2, fold_in)

    acc[...] = pair[own_pair, z % 2].astype(jnp.float32)

    def z_land(s):
        sender = (z + s) % RING

        @pl.when((plane == 0) | (sender > z))
        def _():
            remote(zbuf.at[sender], zbuf.at[sender], send_z2.at[0], recv_z2.at[sender],
                   ctx=ctx_of(plane, sender, core)).wait_recv()
            acc[...] += zbuf[sender].astype(jnp.float32)

    loop(1, RING, z_land)
    kg_ref[0] = acc[:, :HDIM].astype(jnp.bfloat16)
    vg_ref[0] = acc[:, HDIM:].astype(jnp.bfloat16)

    loop(1, groups, lambda s: o_copy(s).wait_recv())
    for t in range(slots):
        moved_ref[t] = landed_o[plan_ref[0, t]]

    def exchanged(s):
        g_copy(s).wait_send()
        o_copy(s).wait_send()

    loop(1, groups, exchanged)
    first_copy(1, True).wait_send()
    first_copy(1, False).wait_send()
    loop(1, RING - 2, lambda i: r_copy(1, i).wait_send())

    @pl.when(plane == 0)
    def _():
        x_copy(1, 0).wait_send()

    @pl.when(plane == 1)
    def _():
        first_copy(2, True).wait_send()
        first_copy(2, False).wait_send()
        loop(1, RING - 2, lambda i: r_copy(2, i).wait_send())

    def gathered(i):
        @pl.when((i >= 1) & goes(i))
        def _():
            f_copy(i).wait_send()

        @pl.when(comes(i))
        def _():
            s_copy(0, plane, i).wait_send()

        s_copy(1, plane, i).wait_send()

        @pl.when(plane == 0)
        def _():
            x_copy(0, i).wait_send()

        @pl.when(plane == 1)
        def _():
            s_copy(0, 0, i).wait_send()
            s_copy(1, 0, i).wait_send()

        @pl.when((i < z) | ((plane == 0) & (i != z)))
        def _():
            z2_copy(i).wait_send()

        @pl.when(i < far)
        def _():
            x2_copy(i).wait_send()

    loop(0, RING, gathered)
    loop(0, own_pair + 1, lambda i: s2_copy(pair_at(i)).wait_send())


def hand_over(moved_in, dq_in, kg_in, vg_in, moved_out, dq_out, kg_out, vg_out):
    moved_out[...] = moved_in[...]
    dq_out[...] = dq_in[...]
    kg_out[...] = kg_in[...]
    vg_out[...] = vg_in[...]


def per_device(queries, key_states, value_states, doc_start, move_plan, out_grad):
    tok, width = queries.shape[1:]
    heads = width // HDIM
    rows = heads * tok
    groups = lax.axis_size("dp")
    pieces = lax.axis_size("ctx")
    slots = move_plan.shape[1]
    block_rows = tok // slots
    tile = CORES * tok
    vmem = pl.BlockSpec(memory_space=pltpu.VMEM)
    smem = pl.BlockSpec(memory_space=pltpu.SMEM)
    bf, f32 = jnp.bfloat16, jnp.float32
    dma = pltpu.SemaphoreType.DMA
    blocks = pltpu.VMEM((groups, block_rows, width), bf)
    heads_bf = pltpu.VMEM((rows, HDIM), bf)

    moved, dq, kg, vg = pl.pallas_call(
        functools.partial(kernel, groups, slots, heads),
        out_shape=(
            jax.ShapeDtypeStruct((slots, block_rows, width), bf),
            jax.ShapeDtypeStruct((tok, width), bf),
            jax.ShapeDtypeStruct((1, tok, HDIM), bf),
            jax.ShapeDtypeStruct((1, tok, HDIM), bf),
        ),
        in_specs=[vmem, vmem, vmem, vmem, smem, vmem],
        out_specs=(vmem,) * 4,
        scratch_shapes=[
            pltpu.VMEM((pieces, tok, HDIM), bf),
            pltpu.VMEM((pieces, tok, HDIM), bf),
            pltpu.VMEM((tok, tok), bf),
            heads_bf, heads_bf, heads_bf, heads_bf,
            pltpu.VMEM((2 * PAIRS, tile, rows), f32),
            pltpu.VMEM((PAIRS, 2 * tile, rows), bf),
            pltpu.VMEM((8, rows), f32),
            pltpu.VMEM((8, rows), f32),
            pltpu.VMEM((HDIM, rows), f32),
            pltpu.VMEM((HDIM, rows), f32),
            pltpu.VMEM((8, rows), f32),
            pltpu.VMEM((slots, block_rows, width), bf),
            blocks, blocks, blocks, blocks,
            pltpu.VMEM((PAIRS, CORES, 2, tok, 2 * HDIM), bf),
            pltpu.VMEM((PAIRS, 2, tok, 2 * HDIM), bf),
            pltpu.VMEM((PAIRS, 2, tok, 2 * HDIM), bf),
            pltpu.VMEM((PAIRS // 2, 2, tok, 2 * HDIM), bf),
            pltpu.VMEM((RING, tok, 2 * HDIM), bf),
            pltpu.VMEM((tok, 2 * HDIM), f32),
            dma((3, RING)), dma((2, RING)), dma((2, 2 * RING)), dma((2, pieces)),
            dma((groups,)), dma((groups,)), dma((groups,)), dma((groups,)),
            dma((PAIRS,)), dma((PAIRS,)), dma((PAIRS // 2,)), dma((PAIRS // 2,)),
            dma((RING,)), dma((RING,)),
        ],
        compiler_params=pltpu.CompilerParams(
            collective_id=0, has_side_effects=True, vmem_limit_bytes=VMEM_LIMIT),
    )(
        queries[0], key_states, value_states, doc_start, move_plan,
        out_grad.reshape(slots, block_rows, width),
    )
    moved, dq, kg, vg = pl.pallas_call(
        hand_over,
        out_shape=tuple(jax.ShapeDtypeStruct(x.shape, x.dtype) for x in (moved, dq, kg, vg)),
        in_specs=[vmem] * 4,
        out_specs=(vmem,) * 4,
    )(moved, dq, kg, vg)
    return moved.reshape(1, tok, width), dq[None], kg, vg


def solution(mesh):
    split = P("dp", "ctx", None)
    return jax.shard_map(
        per_device,
        mesh=mesh,
        in_specs=(split, split, split, P("dp", "ctx"), P("ctx", None), split),
        out_specs=(split, split, split, split),
        check_vma=False,
    )
```

```python
import functools
import math

import jax
import jax.numpy as jnp
from jax import lax
from jax.experimental import pallas as pl
from jax.experimental.pallas import tpu as pltpu
from jax.sharding import PartitionSpec as P

HDIM = 128
MASKED = -1e30
MESH = pl.DeviceIdType.MESH
VMEM_LIMIT = 58 * 1024 * 1024
CORES = 2
RING = 8
PAIRS = 8
NT = (((1,), (1,)), ((), ()))
TN = (((0,), (0,)), ((), ()))
NN = (((1,), (0,)), ((), ()))


def dot(a, b, dims):
    return lax.dot_general(a, b, dims, preferred_element_type=jnp.float32)


def add(a, b):
    return (a.astype(jnp.float32) + b.astype(jnp.float32)).astype(jnp.bfloat16)


def ctx_of(plane, z, core):
    return (plane * RING + z) * CORES + core


def remote(src, dst, send_sem, recv_sem, **axes):
    return pltpu.make_async_remote_copy(
        src_ref=src, dst_ref=dst, send_sem=send_sem, recv_sem=recv_sem,
        device_id=axes, device_id_type=MESH,
    )


def loop(low, high, step):
    def body(i, carry):
        step(i)
        return carry

    lax.fori_loop(low, high, body, 0)


def slot_of(plan_ref, s, slots):
    found = jnp.int32(0)
    for t in range(slots):
        found = jnp.where(plan_ref[0, t] == s, jnp.int32(t), found)
    return found


def kernel(groups, slots, heads,
           q_ref, k_ref, v_ref, starts_ref, plan_ref, grad_ref,
           moved_ref, dq_ref, kg_ref, vg_ref,
           keys_all, values_all, eye, qh, gh, qs, gs, scores, probs, top, total, outT, dqT, dotT, attn,
           stage_g, landed_g, stage_o, landed_o, part, sib, pair, xbuf, zbuf, acc,
           send_f, send_x, send_s, recv_kv, send_g, recv_g, send_o, recv_o,
           send_s2, recv_s2, send_x2, recv_x2, send_z2, recv_z2):
    tok = q_ref.shape[0]
    block_rows = tok // slots
    rows = heads * tok
    tile = CORES * tok
    scale = 1.0 / math.sqrt(HDIM)
    to_two = scale / math.log(2.0)
    group = lax.axis_index("dp")
    ctx = lax.axis_index("ctx")
    chip = ctx // CORES
    plane, z, core = chip // RING, chip % RING, ctx % CORES
    own_pair = chip // 2
    wide = rows // 2
    chunks = [slice(n * wide, (n + 1) * wide) for n in range(2)]

    def flip(x):
        return dot(eye[...], x, NT)

    barrier = pltpu.get_barrier_semaphore()

    def hello(**axes):
        pl.semaphore_signal(barrier, inc=1, device_id=axes, device_id_type=MESH)

    loop(1, groups, lambda s: hello(dp=(group + s) % groups))
    loop(1, RING, lambda s: hello(ctx=ctx_of(plane, (z + s) % RING, core)))
    hello(ctx=ctx_of(1 - plane, z, core))
    hello(ctx=ctx_of(plane, z, 1 - core))

    keys_all[ctx] = k_ref[0]
    values_all[ctx] = v_ref[0]
    for s in range(groups):
        block = grad_ref[slot_of(plan_ref, s, slots)]
        if s == 0:
            landed_g[0] = block
        else:
            stage_g[s] = block
    for h in range(heads):
        qh[h * tok:(h + 1) * tok] = q_ref[:, h * HDIM:(h + 1) * HDIM]
    eye[...] = jnp.where(
        lax.broadcasted_iota(jnp.int32, (tok, tok), 0)
        == lax.broadcasted_iota(jnp.int32, (tok, tok), 1), 1.0, 0.0).astype(jnp.bfloat16)
    top[...] = jnp.full_like(top, MASKED)
    total[...] = jnp.zeros_like(total)
    outT[...] = jnp.zeros_like(outT)
    dqT[...] = jnp.zeros_like(dqT)
    pl.semaphore_wait(barrier, groups - 1 + RING - 1 + 2)

    def offset(i):
        return jnp.where(i == 0, 0, jnp.where(i % 2 == 1, RING // 2 + i // 2, RING // 2 - i // 2))

    def origin(i):
        return (z + RING - offset(i)) % RING

    def goes(i):
        return (plane == 0) | ((z + offset(i)) % RING >= z // 2 * 2)

    def comes(i):
        return (plane == 0) | (origin(i) <= z // 2 * 2 + 1)

    def around(i):
        hop = (i + 1) // 2
        return (z + jnp.where(i % 2 == 1, RING - hop, hop)) % RING

    def stream(kind):
        return (keys_all, 0) if kind == 0 else (values_all, 1)

    def source(kind, i):
        return origin(i) if kind == 0 else around(i)

    def f_copy(i):
        return remote(keys_all.at[ctx], keys_all.at[ctx], send_f.at[0, i], recv_kv.at[0, ctx],
                      ctx=ctx_of(plane, (z + offset(i)) % RING, core))

    def ring_copy(kind, i, sem, ahead):
        block = ctx_of(0 if kind == 2 else plane, around(i), core)
        return remote(values_all.at[block], values_all.at[block], send_f.at[kind, sem],
                      recv_kv.at[1, block],
                      ctx=ctx_of(plane, (z + jnp.where(ahead, 1, RING - 1)) % RING, core))

    def r_copy(kind, i):
        return ring_copy(kind, i, i, i % 2 == 1)

    def first_copy(kind, ahead):
        return ring_copy(kind, 0, 0 if ahead else RING - 1, ahead)

    def x_copy(kind, i):
        buf, which = stream(kind)
        block = ctx_of(0, source(kind, i), core)
        return remote(buf.at[block], buf.at[block], send_x.at[which, i], recv_kv.at[which, block],
                      ctx=ctx_of(1, z, core))

    def s_copy(kind, owner, i):
        buf, which = stream(kind)
        block = ctx_of(owner, source(kind, i), core)
        return remote(buf.at[block], buf.at[block], send_s.at[which, owner * RING + i],
                      recv_kv.at[which, block], ctx=ctx_of(plane, z, 1 - core))

    def g_copy(s):
        return remote(stage_g.at[s], landed_g.at[s], send_g.at[s], recv_g.at[s],
                      dp=(group + groups - s) % groups)

    def o_copy(s):
        return remote(stage_o.at[s], landed_o.at[s], send_o.at[s], recv_o.at[s],
                      dp=(group + s) % groups)

    def arrived(kind, block):
        buf, which = stream(kind)
        remote(buf.at[block], buf.at[block], send_f.at[0, 0], recv_kv.at[which, block],
               ctx=ctx_of(plane, z, 1 - core)).wait_recv()

    for kind in range(2):
        s_copy(kind, plane, 0).start()

        @pl.when(plane == 0)
        def _():
            x_copy(kind, 0).start()

    def spread_out(i):
        @pl.when(goes(i))
        def _():
            f_copy(i).start()

    loop(1, RING, spread_out)
    first_copy(1, True).start()
    first_copy(1, False).start()
    loop(1, groups, lambda s: g_copy(s).start())

    def fold(x):
        return x.reshape(x.shape[0] // 8, 8, x.shape[1])

    def score(n):
        keys = keys_all[pl.ds(CORES * n, CORES)].reshape(tile, HDIM)
        at = n * tile + lax.broadcasted_iota(jnp.int32, (tile, tok), 0)
        mine = ctx * tok + lax.broadcasted_iota(jnp.int32, (tile, tok), 1)
        bias = jnp.where((at >= starts_ref[...]) & (at <= mine), 0.0, MASKED)
        bias = jnp.concatenate([bias] * (wide // tok), axis=1)
        for c in chunks:
            s = dot(keys, qh[c], NT) + bias
            scores[n, :, c] = s
            top[:, c] = jnp.maximum(top[:, c], jnp.max(fold(s), axis=0))

    def gather_step(i):
        @pl.when((i >= 1) & (i < RING))
        def _():
            @pl.when(comes(i))
            def _():
                arrived(0, ctx_of(plane, origin(i), core))

                @pl.when(plane == 0)
                def _():
                    x_copy(0, i).start()

                s_copy(0, plane, i).start()

            arrived(1, ctx_of(plane, around(i), core))

            @pl.when(i < RING - 2)
            def _():
                r_copy(1, i).start()

            s_copy(1, plane, i).start()

        @pl.when((plane == 1) & (i >= 1) & (i <= RING))
        def _():
            j = i - 1
            arrived(0, ctx_of(0, origin(j), core))
            s_copy(0, 0, j).start()
            arrived(1, ctx_of(0, around(j), core))

            @pl.when(j == 0)
            def _():
                first_copy(2, True).start()
                first_copy(2, False).start()

            @pl.when((j >= 1) & (j < RING - 2))
            def _():
                r_copy(2, j).start()

            s_copy(1, 0, j).start()

        @pl.when((i >= 1) & (i <= RING))
        def _():
            near = plane * RING + origin(i - 1)

            @pl.when(comes(i - 1))
            def _():
                arrived(0, CORES * near + 1 - core)

            @pl.when(near <= 2 * own_pair + 1)
            def _():
                score(near)

        @pl.when((plane == 1) & (i >= 2))
        def _():
            arrived(0, CORES * origin(i - 2) + 1 - core)
            score(origin(i - 2))

    loop(0, RING + 2, gather_step)
    top[...] = jnp.broadcast_to(jnp.max(top[...], axis=0, keepdims=True) * to_two, top.shape)

    loop(0, RING, lambda i: arrived(1, ctx_of(plane, i, 1 - core)))

    @pl.when(plane == 1)
    def _():
        loop(0, RING, lambda i: arrived(1, ctx_of(0, i, 1 - core)))

    def weigh(u):
        values = values_all[pl.ds(2 * CORES * u, 2 * CORES)].reshape(2 * tile, HDIM)
        for c in chunks:
            s = scores[pl.ds(2 * u, 2), :, c].reshape(2 * tile, wide)
            p = jnp.exp2(s * to_two - top[0:1, c])
            total[:, c] += jnp.sum(fold(p), axis=0)
            p = p.astype(jnp.bfloat16)
            probs[u, :, c] = p
            outT[:, c] += dot(values, p, TN)

    loop(0, own_pair + 1, weigh)
    inverse = 1.0 / jnp.sum(total[...], axis=0, keepdims=True)
    total[...] = jnp.broadcast_to(inverse, total.shape)
    for h in range(heads):
        mine = slice(h * tok, (h + 1) * tok)
        out = flip((outT[:, mine] * total[0:1, mine]).astype(jnp.bfloat16)).astype(jnp.bfloat16)
        attn[:, :, h * HDIM:(h + 1) * HDIM] = out.reshape(slots, block_rows, HDIM)
    for s in range(groups):
        block = attn[slot_of(plan_ref, s, slots)]
        if s == 0:
            landed_o[0] = block
        else:
            stage_o[s] = block
    loop(1, groups, lambda s: o_copy(s).start())

    loop(1, groups, lambda s: g_copy(s).wait_recv())
    for t in range(slots):
        block = landed_g[plan_ref[0, t]]
        for h in range(heads):
            first = h * tok + t * block_rows
            gh[first:first + block_rows] = block[:, h * HDIM:(h + 1) * HDIM]
    ones = jnp.ones((8, HDIM), jnp.bfloat16)
    for h in range(heads):
        mine = slice(h * tok, (h + 1) * tok)
        out = attn[:, :, h * HDIM:(h + 1) * HDIM].reshape(tok, HDIM)
        grad = gh[mine].astype(jnp.float32)
        prod = grad * out.astype(jnp.float32)
        high = prod.astype(jnp.bfloat16)
        low = (prod - high.astype(jnp.float32)).astype(jnp.bfloat16)
        dotT[:, mine] = dot(ones, high, NT) + dot(ones, low, NT)
        spread = jnp.broadcast_to(total[0:1, mine], (HDIM, tok))
        coarse = spread.astype(jnp.bfloat16)
        fine = (spread - coarse.astype(jnp.float32)).astype(jnp.bfloat16)
        back = flip(coarse) + flip(fine)
        gs[mine] = (grad * back).astype(jnp.bfloat16)
        qs[mine] = (qh[mine].astype(jnp.float32) * (back * scale)).astype(jnp.bfloat16)

    far = plane * (PAIRS // 2)

    near_pairs = z // 2 + 1

    def far_pair(turn):
        flip_way = (turn == 1) == (z // 2 % 2 == 0)
        step = jnp.where(turn == 0, 2, jnp.where(turn == 3, 0, jnp.where(flip_way, 1, 3)))
        return (z // 2 + step) % (PAIRS // 2)

    def pair_at(i):
        away = (plane == 1) & ((i % 2 == 0) | (i >= 2 * near_pairs))
        turn = jnp.where(i < 2 * near_pairs, i // 2, i - near_pairs)
        near = (2 * near_pairs - 2 - jnp.where(plane == 1, turn, i)) % near_pairs
        return jnp.where(away, far_pair(turn), far + near)

    def s2_copy(u):
        return remote(part.at[u, 1 - core], sib.at[u], send_s2.at[u], recv_s2.at[u],
                      ctx=ctx_of(plane, z, 1 - core))

    def x2_copy(spot):
        u, which = spot // 2, spot % 2
        return remote(pair.at[u, which], xbuf.at[u, which], send_x2.at[spot], recv_x2.at[spot],
                      ctx=ctx_of(1 - plane, z, core))

    def z2_copy(spot):
        return remote(pair.at[far + spot // 2, spot % 2], zbuf.at[z], send_z2.at[spot],
                      recv_z2.at[z], ctx=ctx_of(plane, spot, core))

    def back(u):
        keys = keys_all[pl.ds(2 * CORES * u, 2 * CORES)].reshape(2 * tile, HDIM)
        values = values_all[pl.ds(2 * CORES * u, 2 * CORES)].reshape(2 * tile, HDIM)
        dp = dot(values, gh[...], NT)
        p = probs[u]
        ds = (p.astype(jnp.float32) * (dp - dotT[0:1])).astype(jnp.bfloat16)
        dqT[...] += dot(keys, ds, TN)
        dk = dot(ds, qs[...], NN).astype(jnp.bfloat16)
        dv = dot(p, gs[...], NN).astype(jnp.bfloat16)
        for which in range(2):
            for c in range(CORES):
                first = (which * CORES + c) * tok
                part[u, c, which, :, :HDIM] = dk[first:first + tok]
                part[u, c, which, :, HDIM:] = dv[first:first + tok]

    def pass_on(u):
        s2_copy(u).wait_recv()
        pair[u] = add(part[u, core], sib[u])

        @pl.when(u < far)
        def _():
            x2_copy(2 * u).start()
            x2_copy(2 * u + 1).start()

        @pl.when((plane == 1) & (u >= far))
        def _():
            for which in range(2):
                spot = (u - far) * 2 + which

                @pl.when(spot < z)
                def _():
                    z2_copy(spot).start()

    def back_step(i):
        u = pair_at(i)
        back(u)
        s2_copy(u).start()

        @pl.when(i >= 1)
        def _():
            pass_on(pair_at(i - 1))

    loop(0, own_pair + 1, back_step)
    pass_on(pair_at(own_pair))

    for h in range(heads):
        mine = slice(h * tok, (h + 1) * tok)
        dq_ref[:, h * HDIM:(h + 1) * HDIM] = flip(
            (dqT[:, mine] * (total[0:1, mine] * scale)).astype(jnp.bfloat16)).astype(jnp.bfloat16)

    @pl.when(plane == 0)
    def _():
        def fold_in(j):
            u = far_pair(j)
            for which in range(2):
                spot = u * 2 + which
                x2_copy(spot).wait_recv()

                @pl.when(u <= own_pair)
                def _():
                    pair[u, which] = add(pair[u, which], xbuf[u, which])

                @pl.when(u > own_pair)
                def _():
                    pair[u, which] = xbuf[u, which]

                @pl.when(spot != z)
                def _():
                    z2_copy(spot).start()

        loop(0, PAIRS // 2, fold_in)

    acc[...] = pair[own_pair, z % 2].astype(jnp.float32)

    def z_land(s):
        sender = (z + s) % RING

        @pl.when((plane == 0) | (sender > z))
        def _():
            remote(zbuf.at[sender], zbuf.at[sender], send_z2.at[0], recv_z2.at[sender],
                   ctx=ctx_of(plane, sender, core)).wait_recv()
            acc[...] += zbuf[sender].astype(jnp.float32)

    loop(1, RING, z_land)
    kg_ref[0] = acc[:, :HDIM].astype(jnp.bfloat16)
    vg_ref[0] = acc[:, HDIM:].astype(jnp.bfloat16)

    loop(1, groups, lambda s: o_copy(s).wait_recv())
    for t in range(slots):
        moved_ref[t] = landed_o[plan_ref[0, t]]

    def exchanged(s):
        g_copy(s).wait_send()
        o_copy(s).wait_send()

    loop(1, groups, exchanged)
    first_copy(1, True).wait_send()
    first_copy(1, False).wait_send()
    loop(1, RING - 2, lambda i: r_copy(1, i).wait_send())

    @pl.when(plane == 0)
    def _():
        x_copy(1, 0).wait_send()

    @pl.when(plane == 1)
    def _():
        first_copy(2, True).wait_send()
        first_copy(2, False).wait_send()
        loop(1, RING - 2, lambda i: r_copy(2, i).wait_send())

    def gathered(i):
        @pl.when((i >= 1) & goes(i))
        def _():
            f_copy(i).wait_send()

        @pl.when(comes(i))
        def _():
            s_copy(0, plane, i).wait_send()

        s_copy(1, plane, i).wait_send()

        @pl.when(plane == 0)
        def _():
            x_copy(0, i).wait_send()

        @pl.when(plane == 1)
        def _():
            s_copy(0, 0, i).wait_send()
            s_copy(1, 0, i).wait_send()

        @pl.when((i < z) | ((plane == 0) & (i != z)))
        def _():
            z2_copy(i).wait_send()

        @pl.when(plane == 1)
        def _():
            x2_copy(i).wait_send()

    loop(0, RING, gathered)
    loop(0, own_pair + 1, lambda i: s2_copy(pair_at(i)).wait_send())


def hand_over(moved_in, dq_in, kg_in, vg_in, moved_out, dq_out, kg_out, vg_out):
    moved_out[...] = moved_in[...]
    dq_out[...] = dq_in[...]
    kg_out[...] = kg_in[...]
    vg_out[...] = vg_in[...]


def per_device(queries, key_states, value_states, doc_start, move_plan, out_grad):
    tok, width = queries.shape[1:]
    heads = width // HDIM
    rows = heads * tok
    groups = lax.axis_size("dp")
    pieces = lax.axis_size("ctx")
    slots = move_plan.shape[1]
    block_rows = tok // slots
    tile = CORES * tok
    vmem = pl.BlockSpec(memory_space=pltpu.VMEM)
    smem = pl.BlockSpec(memory_space=pltpu.SMEM)
    bf, f32 = jnp.bfloat16, jnp.float32
    dma = pltpu.SemaphoreType.DMA
    blocks = pltpu.VMEM((groups, block_rows, width), bf)
    heads_bf = pltpu.VMEM((rows, HDIM), bf)

    moved, dq, kg, vg = pl.pallas_call(
        functools.partial(kernel, groups, slots, heads),
        out_shape=(
            jax.ShapeDtypeStruct((slots, block_rows, width), bf),
            jax.ShapeDtypeStruct((tok, width), bf),
            jax.ShapeDtypeStruct((1, tok, HDIM), bf),
            jax.ShapeDtypeStruct((1, tok, HDIM), bf),
        ),
        in_specs=[vmem, vmem, vmem, vmem, smem, vmem],
        out_specs=(vmem,) * 4,
        scratch_shapes=[
            pltpu.VMEM((pieces, tok, HDIM), bf),
            pltpu.VMEM((pieces, tok, HDIM), bf),
            pltpu.VMEM((tok, tok), bf),
            heads_bf, heads_bf, heads_bf, heads_bf,
            pltpu.VMEM((2 * PAIRS, tile, rows), f32),
            pltpu.VMEM((PAIRS, 2 * tile, rows), bf),
            pltpu.VMEM((8, rows), f32),
            pltpu.VMEM((8, rows), f32),
            pltpu.VMEM((HDIM, rows), f32),
            pltpu.VMEM((HDIM, rows), f32),
            pltpu.VMEM((8, rows), f32),
            pltpu.VMEM((slots, block_rows, width), bf),
            blocks, blocks, blocks, blocks,
            pltpu.VMEM((PAIRS, CORES, 2, tok, 2 * HDIM), bf),
            pltpu.VMEM((PAIRS, 2, tok, 2 * HDIM), bf),
            pltpu.VMEM((PAIRS, 2, tok, 2 * HDIM), bf),
            pltpu.VMEM((PAIRS // 2, 2, tok, 2 * HDIM), bf),
            pltpu.VMEM((RING, tok, 2 * HDIM), bf),
            pltpu.VMEM((tok, 2 * HDIM), f32),
            dma((3, RING)), dma((2, RING)), dma((2, 2 * RING)), dma((2, pieces)),
            dma((groups,)), dma((groups,)), dma((groups,)), dma((groups,)),
            dma((PAIRS,)), dma((PAIRS,)), dma((RING,)), dma((RING,)),
            dma((RING,)), dma((RING,)),
        ],
        compiler_params=pltpu.CompilerParams(
            collective_id=0, has_side_effects=True, vmem_limit_bytes=VMEM_LIMIT),
    )(
        queries[0], key_states, value_states, doc_start, move_plan,
        out_grad.reshape(slots, block_rows, width),
    )
    moved, dq, kg, vg = pl.pallas_call(
        hand_over,
        out_shape=tuple(jax.ShapeDtypeStruct(x.shape, x.dtype) for x in (moved, dq, kg, vg)),
        in_specs=[vmem] * 4,
        out_specs=(vmem,) * 4,
    )(moved, dq, kg, vg)
    return moved.reshape(1, tok, width), dq[None], kg, vg


def solution(mesh):
    split = P("dp", "ctx", None)
    return jax.shard_map(
        per_device,
        mesh=mesh,
        in_specs=(split, split, split, P("dp", "ctx"), P("ctx", None), split),
        out_specs=(split, split, split, split),
        check_vma=False,
    )
```

```python
import functools
import math

import jax
import jax.numpy as jnp
from jax import lax
from jax.experimental import pallas as pl
from jax.experimental.pallas import tpu as pltpu
from jax.sharding import PartitionSpec as P

HDIM = 128
MASKED = -1e30
MESH = pl.DeviceIdType.MESH
VMEM_LIMIT = 58 * 1024 * 1024
CORES = 2
RING = 8
PAIRS = 8
NT = (((1,), (1,)), ((), ()))
TN = (((0,), (0,)), ((), ()))
NN = (((1,), (0,)), ((), ()))


def dot(a, b, dims):
    return lax.dot_general(a, b, dims, preferred_element_type=jnp.float32)


def add(a, b):
    return (a.astype(jnp.float32) + b.astype(jnp.float32)).astype(jnp.bfloat16)


def ctx_of(plane, z, core):
    return (plane * RING + z) * CORES + core


def remote(src, dst, send_sem, recv_sem, **axes):
    return pltpu.make_async_remote_copy(
        src_ref=src, dst_ref=dst, send_sem=send_sem, recv_sem=recv_sem,
        device_id=axes, device_id_type=MESH,
    )


def loop(low, high, step):
    def body(i, carry):
        step(i)
        return carry

    lax.fori_loop(low, high, body, 0)


def slot_of(plan_ref, s, slots):
    found = jnp.int32(0)
    for t in range(slots):
        found = jnp.where(plan_ref[0, t] == s, jnp.int32(t), found)
    return found


def kernel(groups, slots, heads,
           q_ref, k_ref, v_ref, starts_ref, plan_ref, grad_ref,
           moved_ref, dq_ref, kg_ref, vg_ref,
           keys_all, values_all, eye, qh, gh, qs, gs, scores, probs, top, total, outT, dqT, dotT, attn,
           stage_g, landed_g, stage_o, landed_o, part, sib, pair, xbuf, zbuf, acc,
           send_f, send_x, send_s, recv_kv, send_g, recv_g, send_o, recv_o,
           send_s2, recv_s2, send_x2, recv_x2, send_z2, recv_z2):
    tok = q_ref.shape[0]
    block_rows = tok // slots
    rows = heads * tok
    tile = CORES * tok
    scale = 1.0 / math.sqrt(HDIM)
    to_two = scale / math.log(2.0)
    group = lax.axis_index("dp")
    ctx = lax.axis_index("ctx")
    chip = ctx // CORES
    plane, z, core = chip // RING, chip % RING, ctx % CORES
    own_pair = chip // 2
    wide = rows // 2
    chunks = [slice(n * wide, (n + 1) * wide) for n in range(2)]

    def flip(x):
        return dot(eye[...], x, NT)

    barrier = pltpu.get_barrier_semaphore()

    def hello(**axes):
        pl.semaphore_signal(barrier, inc=1, device_id=axes, device_id_type=MESH)

    loop(1, groups, lambda s: hello(dp=(group + s) % groups))
    loop(1, RING, lambda s: hello(ctx=ctx_of(plane, (z + s) % RING, core)))
    hello(ctx=ctx_of(1 - plane, z, core))
    hello(ctx=ctx_of(plane, z, 1 - core))

    keys_all[ctx] = k_ref[0]
    values_all[ctx] = v_ref[0]
    for s in range(groups):
        block = grad_ref[slot_of(plan_ref, s, slots)]
        if s == 0:
            landed_g[0] = block
        else:
            stage_g[s] = block
    for h in range(heads):
        qh[h * tok:(h + 1) * tok] = q_ref[:, h * HDIM:(h + 1) * HDIM]
    eye[...] = jnp.where(
        lax.broadcasted_iota(jnp.int32, (tok, tok), 0)
        == lax.broadcasted_iota(jnp.int32, (tok, tok), 1), 1.0, 0.0).astype(jnp.bfloat16)
    top[...] = jnp.full_like(top, MASKED)
    total[...] = jnp.zeros_like(total)
    outT[...] = jnp.zeros_like(outT)
    dqT[...] = jnp.zeros_like(dqT)
    pl.semaphore_wait(barrier, groups - 1 + RING - 1 + 2)

    def origin(i):
        hop = (i + 1) // 2
        return (z + jnp.where(i % 2 == 1, RING - hop, hop)) % RING

    def stream(kind):
        return (keys_all, 0) if kind == 0 else (values_all, 1)

    def ring_copy(kind, i, sem, ahead):
        buf, which = stream(kind)
        block = ctx_of(0 if kind == 2 else plane, origin(i), core)
        return remote(buf.at[block], buf.at[block], send_f.at[kind, sem], recv_kv.at[which, block],
                      ctx=ctx_of(plane, (z + jnp.where(ahead, 1, RING - 1)) % RING, core))

    def f_copy(kind, i):
        return ring_copy(kind, i, i, i % 2 == 1)

    def first_copy(kind, ahead):
        return ring_copy(kind, 0, 0 if ahead else RING - 1, ahead)

    def x_copy(kind, i):
        buf, which = stream(kind)
        block = ctx_of(0, origin(i), core)
        return remote(buf.at[block], buf.at[block], send_x.at[which, i], recv_kv.at[which, block],
                      ctx=ctx_of(1, z, core))

    def s_copy(kind, owner, i):
        buf, which = stream(kind)
        block = ctx_of(owner, origin(i), core)
        return remote(buf.at[block], buf.at[block], send_s.at[which, owner * RING + i],
                      recv_kv.at[which, block], ctx=ctx_of(plane, z, 1 - core))

    def g_copy(s):
        return remote(stage_g.at[s], landed_g.at[s], send_g.at[s], recv_g.at[s],
                      dp=(group + groups - s) % groups)

    def o_copy(s):
        return remote(stage_o.at[s], landed_o.at[s], send_o.at[s], recv_o.at[s],
                      dp=(group + s) % groups)

    def arrived(kind, block):
        buf, which = stream(kind)
        remote(buf.at[block], buf.at[block], send_f.at[0, 0], recv_kv.at[which, block],
               ctx=ctx_of(plane, z, 1 - core)).wait_recv()

    for kind in range(2):
        first_copy(kind, True).start()
        first_copy(kind, False).start()

        @pl.when(plane == 0)
        def _():
            x_copy(kind, 0).start()

        s_copy(kind, plane, 0).start()

    loop(1, groups, lambda s: g_copy(s).start())

    def fold(x):
        return x.reshape(x.shape[0] // 8, 8, x.shape[1])

    def score(n):
        keys = keys_all[pl.ds(CORES * n, CORES)].reshape(tile, HDIM)
        at = n * tile + lax.broadcasted_iota(jnp.int32, (tile, tok), 0)
        mine = ctx * tok + lax.broadcasted_iota(jnp.int32, (tile, tok), 1)
        bias = jnp.where((at >= starts_ref[...]) & (at <= mine), 0.0, MASKED)
        bias = jnp.concatenate([bias] * (wide // tok), axis=1)
        for c in chunks:
            s = dot(keys, qh[c], NT) + bias
            scores[n, :, c] = s
            top[:, c] = jnp.maximum(top[:, c], jnp.max(fold(s), axis=0))

    def gather_step(i):
        @pl.when((i >= 1) & (i < RING))
        def _():
            for kind in range(2):
                arrived(kind, ctx_of(plane, origin(i), core))

                @pl.when(i < RING - 2)
                def _():
                    f_copy(kind, i).start()

                if kind == 0:
                    @pl.when(plane == 0)
                    def _():
                        x_copy(0, i).start()

                s_copy(kind, plane, i).start()

        @pl.when((plane == 1) & (i >= 1) & (i <= RING))
        def _():
            j = i - 1
            for kind in (0, 2):
                arrived(kind, ctx_of(0, origin(j), core))
                if kind == 2:
                    @pl.when(j == 0)
                    def _():
                        first_copy(2, True).start()
                        first_copy(2, False).start()

                    @pl.when((j >= 1) & (j < RING - 2))
                    def _():
                        f_copy(2, j).start()

                s_copy(kind, 0, j).start()

        @pl.when((i >= 1) & (i <= RING))
        def _():
            near = plane * RING + origin(i - 1)
            arrived(0, CORES * near + 1 - core)

            @pl.when(near <= 2 * own_pair + 1)
            def _():
                score(near)

        @pl.when((plane == 1) & (i >= 2))
        def _():
            arrived(0, CORES * origin(i - 2) + 1 - core)
            score(origin(i - 2))

    loop(0, RING + 2, gather_step)
    top[...] = jnp.broadcast_to(jnp.max(top[...], axis=0, keepdims=True) * to_two, top.shape)

    loop(0, RING, lambda i: arrived(1, ctx_of(plane, i, 1 - core)))

    @pl.when(plane == 1)
    def _():
        loop(0, RING, lambda i: arrived(1, ctx_of(0, i, 1 - core)))

    def weigh(u):
        values = values_all[pl.ds(2 * CORES * u, 2 * CORES)].reshape(2 * tile, HDIM)
        for c in chunks:
            s = scores[pl.ds(2 * u, 2), :, c].reshape(2 * tile, wide)
            p = jnp.exp2(s * to_two - top[0:1, c])
            total[:, c] += jnp.sum(fold(p), axis=0)
            p = p.astype(jnp.bfloat16)
            probs[u, :, c] = p
            outT[:, c] += dot(values, p, TN)

    loop(0, own_pair + 1, weigh)
    inverse = 1.0 / jnp.sum(total[...], axis=0, keepdims=True)
    total[...] = jnp.broadcast_to(inverse, total.shape)
    for h in range(heads):
        mine = slice(h * tok, (h + 1) * tok)
        out = flip((outT[:, mine] * total[0:1, mine]).astype(jnp.bfloat16)).astype(jnp.bfloat16)
        attn[:, :, h * HDIM:(h + 1) * HDIM] = out.reshape(slots, block_rows, HDIM)
    for s in range(groups):
        block = attn[slot_of(plan_ref, s, slots)]
        if s == 0:
            landed_o[0] = block
        else:
            stage_o[s] = block
    loop(1, groups, lambda s: o_copy(s).start())

    loop(1, groups, lambda s: g_copy(s).wait_recv())
    for t in range(slots):
        block = landed_g[plan_ref[0, t]]
        for h in range(heads):
            first = h * tok + t * block_rows
            gh[first:first + block_rows] = block[:, h * HDIM:(h + 1) * HDIM]
    ones = jnp.ones((8, HDIM), jnp.bfloat16)
    for h in range(heads):
        mine = slice(h * tok, (h + 1) * tok)
        out = attn[:, :, h * HDIM:(h + 1) * HDIM].reshape(tok, HDIM)
        grad = gh[mine].astype(jnp.float32)
        prod = grad * out.astype(jnp.float32)
        high = prod.astype(jnp.bfloat16)
        low = (prod - high.astype(jnp.float32)).astype(jnp.bfloat16)
        dotT[:, mine] = dot(ones, high, NT) + dot(ones, low, NT)
        spread = jnp.broadcast_to(total[0:1, mine], (HDIM, tok))
        coarse = spread.astype(jnp.bfloat16)
        fine = (spread - coarse.astype(jnp.float32)).astype(jnp.bfloat16)
        back = flip(coarse) + flip(fine)
        gs[mine] = (grad * back).astype(jnp.bfloat16)
        qs[mine] = (qh[mine].astype(jnp.float32) * (back * scale)).astype(jnp.bfloat16)

    far = plane * (PAIRS // 2)

    near_pairs = z // 2 + 1

    def far_pair(turn):
        flip_way = (turn == 1) == (z // 2 % 2 == 0)
        step = jnp.where(turn == 0, 2, jnp.where(turn == 3, 0, jnp.where(flip_way, 1, 3)))
        return (z // 2 + step) % (PAIRS // 2)

    def pair_at(i):
        away = (plane == 1) & ((i % 2 == 0) | (i >= 2 * near_pairs))
        turn = jnp.where(i < 2 * near_pairs, i // 2, i - near_pairs)
        near = (2 * near_pairs - 2 - jnp.where(plane == 1, turn, i)) % near_pairs
        return jnp.where(away, far_pair(turn), far + near)

    def s2_copy(u):
        return remote(part.at[u, 1 - core], sib.at[u], send_s2.at[u], recv_s2.at[u],
                      ctx=ctx_of(plane, z, 1 - core))

    def x2_copy(spot):
        u, which = spot // 2, spot % 2
        return remote(pair.at[u, which], xbuf.at[u, which], send_x2.at[spot], recv_x2.at[spot],
                      ctx=ctx_of(1 - plane, z, core))

    def z2_copy(spot):
        return remote(pair.at[far + spot // 2, spot % 2], zbuf.at[z], send_z2.at[spot],
                      recv_z2.at[z], ctx=ctx_of(plane, spot, core))

    def back(u):
        keys = keys_all[pl.ds(2 * CORES * u, 2 * CORES)].reshape(2 * tile, HDIM)
        values = values_all[pl.ds(2 * CORES * u, 2 * CORES)].reshape(2 * tile, HDIM)
        dp = dot(values, gh[...], NT)
        p = probs[u]
        ds = (p.astype(jnp.float32) * (dp - dotT[0:1])).astype(jnp.bfloat16)
        dqT[...] += dot(keys, ds, TN)
        dk = dot(ds, qs[...], NN).astype(jnp.bfloat16)
        dv = dot(p, gs[...], NN).astype(jnp.bfloat16)
        for which in range(2):
            for c in range(CORES):
                first = (which * CORES + c) * tok
                part[u, c, which, :, :HDIM] = dk[first:first + tok]
                part[u, c, which, :, HDIM:] = dv[first:first + tok]

    def pass_on(u):
        s2_copy(u).wait_recv()
        pair[u] = add(part[u, core], sib[u])

        @pl.when(u < far)
        def _():
            x2_copy(2 * u).start()
            x2_copy(2 * u + 1).start()

        @pl.when((plane == 1) & (u >= far))
        def _():
            for which in range(2):
                spot = (u - far) * 2 + which

                @pl.when(spot < z)
                def _():
                    z2_copy(spot).start()

    def back_step(i):
        u = pair_at(i)
        back(u)
        s2_copy(u).start()

        @pl.when(i >= 1)
        def _():
            pass_on(pair_at(i - 1))

    loop(0, own_pair + 1, back_step)
    pass_on(pair_at(own_pair))

    for h in range(heads):
        mine = slice(h * tok, (h + 1) * tok)
        dq_ref[:, h * HDIM:(h + 1) * HDIM] = flip(
            (dqT[:, mine] * (total[0:1, mine] * scale)).astype(jnp.bfloat16)).astype(jnp.bfloat16)

    @pl.when(plane == 0)
    def _():
        def fold_in(j):
            u = far_pair(j)
            for which in range(2):
                spot = u * 2 + which
                x2_copy(spot).wait_recv()

                @pl.when(u <= own_pair)
                def _():
                    pair[u, which] = add(pair[u, which], xbuf[u, which])

                @pl.when(u > own_pair)
                def _():
                    pair[u, which] = xbuf[u, which]

                @pl.when(spot != z)
                def _():
                    z2_copy(spot).start()

        loop(0, PAIRS // 2, fold_in)

    acc[...] = pair[own_pair, z % 2].astype(jnp.float32)

    def z_land(s):
        source = (z + s) % RING

        @pl.when((plane == 0) | (source > z))
        def _():
            remote(zbuf.at[source], zbuf.at[source], send_z2.at[0], recv_z2.at[source],
                   ctx=ctx_of(plane, source, core)).wait_recv()
            acc[...] += zbuf[source].astype(jnp.float32)

    loop(1, RING, z_land)
    kg_ref[0] = acc[:, :HDIM].astype(jnp.bfloat16)
    vg_ref[0] = acc[:, HDIM:].astype(jnp.bfloat16)

    loop(1, groups, lambda s: o_copy(s).wait_recv())
    for t in range(slots):
        moved_ref[t] = landed_o[plan_ref[0, t]]

    def exchanged(s):
        g_copy(s).wait_send()
        o_copy(s).wait_send()

    loop(1, groups, exchanged)
    for kind in range(2):
        first_copy(kind, True).wait_send()
        first_copy(kind, False).wait_send()
        loop(1, RING - 2, lambda i: f_copy(kind, i).wait_send())

    @pl.when(plane == 0)
    def _():
        x_copy(1, 0).wait_send()

    @pl.when(plane == 1)
    def _():
        first_copy(2, True).wait_send()
        first_copy(2, False).wait_send()
        loop(1, RING - 2, lambda i: f_copy(2, i).wait_send())

    def gathered(i):
        for kind in range(2):
            s_copy(kind, plane, i).wait_send()

        @pl.when(plane == 0)
        def _():
            x_copy(0, i).wait_send()

        @pl.when(plane == 1)
        def _():
            s_copy(0, 0, i).wait_send()
            s_copy(1, 0, i).wait_send()

        @pl.when((i < z) | ((plane == 0) & (i != z)))
        def _():
            z2_copy(i).wait_send()

        @pl.when(plane == 1)
        def _():
            x2_copy(i).wait_send()

    loop(0, RING, gathered)
    loop(0, own_pair + 1, lambda i: s2_copy(pair_at(i)).wait_send())


def hand_over(moved_in, dq_in, kg_in, vg_in, moved_out, dq_out, kg_out, vg_out):
    moved_out[...] = moved_in[...]
    dq_out[...] = dq_in[...]
    kg_out[...] = kg_in[...]
    vg_out[...] = vg_in[...]


def per_device(queries, key_states, value_states, doc_start, move_plan, out_grad):
    tok, width = queries.shape[1:]
    heads = width // HDIM
    rows = heads * tok
    groups = lax.axis_size("dp")
    pieces = lax.axis_size("ctx")
    slots = move_plan.shape[1]
    block_rows = tok // slots
    tile = CORES * tok
    vmem = pl.BlockSpec(memory_space=pltpu.VMEM)
    smem = pl.BlockSpec(memory_space=pltpu.SMEM)
    bf, f32 = jnp.bfloat16, jnp.float32
    dma = pltpu.SemaphoreType.DMA
    blocks = pltpu.VMEM((groups, block_rows, width), bf)
    heads_bf = pltpu.VMEM((rows, HDIM), bf)

    moved, dq, kg, vg = pl.pallas_call(
        functools.partial(kernel, groups, slots, heads),
        out_shape=(
            jax.ShapeDtypeStruct((slots, block_rows, width), bf),
            jax.ShapeDtypeStruct((tok, width), bf),
            jax.ShapeDtypeStruct((1, tok, HDIM), bf),
            jax.ShapeDtypeStruct((1, tok, HDIM), bf),
        ),
        in_specs=[vmem, vmem, vmem, vmem, smem, vmem],
        out_specs=(vmem,) * 4,
        scratch_shapes=[
            pltpu.VMEM((pieces, tok, HDIM), bf),
            pltpu.VMEM((pieces, tok, HDIM), bf),
            pltpu.VMEM((tok, tok), bf),
            heads_bf, heads_bf, heads_bf, heads_bf,
            pltpu.VMEM((2 * PAIRS, tile, rows), f32),
            pltpu.VMEM((PAIRS, 2 * tile, rows), bf),
            pltpu.VMEM((8, rows), f32),
            pltpu.VMEM((8, rows), f32),
            pltpu.VMEM((HDIM, rows), f32),
            pltpu.VMEM((HDIM, rows), f32),
            pltpu.VMEM((8, rows), f32),
            pltpu.VMEM((slots, block_rows, width), bf),
            blocks, blocks, blocks, blocks,
            pltpu.VMEM((PAIRS, CORES, 2, tok, 2 * HDIM), bf),
            pltpu.VMEM((PAIRS, 2, tok, 2 * HDIM), bf),
            pltpu.VMEM((PAIRS, 2, tok, 2 * HDIM), bf),
            pltpu.VMEM((PAIRS // 2, 2, tok, 2 * HDIM), bf),
            pltpu.VMEM((RING, tok, 2 * HDIM), bf),
            pltpu.VMEM((tok, 2 * HDIM), f32),
            dma((3, RING)), dma((2, RING)), dma((2, 2 * RING)), dma((2, pieces)),
            dma((groups,)), dma((groups,)), dma((groups,)), dma((groups,)),
            dma((PAIRS,)), dma((PAIRS,)), dma((RING,)), dma((RING,)),
            dma((RING,)), dma((RING,)),
        ],
        compiler_params=pltpu.CompilerParams(
            collective_id=0, has_side_effects=True, vmem_limit_bytes=VMEM_LIMIT),
    )(
        queries[0], key_states, value_states, doc_start, move_plan,
        out_grad.reshape(slots, block_rows, width),
    )
    moved, dq, kg, vg = pl.pallas_call(
        hand_over,
        out_shape=tuple(jax.ShapeDtypeStruct(x.shape, x.dtype) for x in (moved, dq, kg, vg)),
        in_specs=[vmem] * 4,
        out_specs=(vmem,) * 4,
    )(moved, dq, kg, vg)
    return moved.reshape(1, tok, width), dq[None], kg, vg


def solution(mesh):
    split = P("dp", "ctx", None)
    return jax.shard_map(
        per_device,
        mesh=mesh,
        in_specs=(split, split, split, P("dp", "ctx"), P("ctx", None), split),
        out_specs=(split, split, split, split),
        check_vma=False,
    )
```

```python
import functools
import math

import jax
import jax.numpy as jnp
from jax import lax
from jax.experimental import pallas as pl
from jax.experimental.pallas import tpu as pltpu
from jax.sharding import PartitionSpec as P

HDIM = 128
MASKED = -1e30
MESH = pl.DeviceIdType.MESH
VMEM_LIMIT = 58 * 1024 * 1024
CORES = 2
RING = 8
PAIRS = 8
NT = (((1,), (1,)), ((), ()))
TN = (((0,), (0,)), ((), ()))
NN = (((1,), (0,)), ((), ()))


def dot(a, b, dims):
    return lax.dot_general(a, b, dims, preferred_element_type=jnp.float32)


def add(a, b):
    return (a.astype(jnp.float32) + b.astype(jnp.float32)).astype(jnp.bfloat16)


def ctx_of(plane, z, core):
    return (plane * RING + z) * CORES + core


def remote(src, dst, send_sem, recv_sem, **axes):
    return pltpu.make_async_remote_copy(
        src_ref=src, dst_ref=dst, send_sem=send_sem, recv_sem=recv_sem,
        device_id=axes, device_id_type=MESH,
    )


def loop(low, high, step):
    def body(i, carry):
        step(i)
        return carry

    lax.fori_loop(low, high, body, 0)


def slot_of(plan_ref, s, slots):
    found = jnp.int32(0)
    for t in range(slots):
        found = jnp.where(plan_ref[0, t] == s, jnp.int32(t), found)
    return found


def kernel(groups, slots, heads,
           q_ref, k_ref, v_ref, starts_ref, plan_ref, grad_ref,
           moved_ref, dq_ref, kg_ref, vg_ref,
           keys_all, values_all, eye, qh, gh, qs, gs, scores, probs, top, total, outT, dqT, dotT, attn,
           stage_g, landed_g, stage_o, landed_o, part, sib, pair, xbuf, zbuf, acc,
           send_f, send_x, send_s, recv_kv, send_g, recv_g, send_o, recv_o,
           send_s2, recv_s2, send_x2, recv_x2, send_z2, recv_z2):
    tok = q_ref.shape[0]
    block_rows = tok // slots
    rows = heads * tok
    tile = CORES * tok
    scale = 1.0 / math.sqrt(HDIM)
    to_two = scale / math.log(2.0)
    group = lax.axis_index("dp")
    ctx = lax.axis_index("ctx")
    chip = ctx // CORES
    plane, z, core = chip // RING, chip % RING, ctx % CORES
    own_pair = chip // 2
    wide = rows // 2
    chunks = [slice(n * wide, (n + 1) * wide) for n in range(2)]

    def flip(x):
        return dot(eye[...], x, NT)

    barrier = pltpu.get_barrier_semaphore()

    def hello(**axes):
        pl.semaphore_signal(barrier, inc=1, device_id=axes, device_id_type=MESH)

    loop(1, groups, lambda s: hello(dp=(group + s) % groups))
    loop(1, RING, lambda s: hello(ctx=ctx_of(plane, (z + s) % RING, core)))
    hello(ctx=ctx_of(1 - plane, z, core))
    hello(ctx=ctx_of(plane, z, 1 - core))

    keys_all[ctx] = k_ref[0]
    values_all[ctx] = v_ref[0]
    for s in range(groups):
        block = grad_ref[slot_of(plan_ref, s, slots)]
        if s == 0:
            landed_g[0] = block
        else:
            stage_g[s] = block
    for h in range(heads):
        qh[h * tok:(h + 1) * tok] = q_ref[:, h * HDIM:(h + 1) * HDIM]
    eye[...] = jnp.where(
        lax.broadcasted_iota(jnp.int32, (tok, tok), 0)
        == lax.broadcasted_iota(jnp.int32, (tok, tok), 1), 1.0, 0.0).astype(jnp.bfloat16)
    top[...] = jnp.full_like(top, MASKED)
    total[...] = jnp.zeros_like(total)
    outT[...] = jnp.zeros_like(outT)
    dqT[...] = jnp.zeros_like(dqT)
    pl.semaphore_wait(barrier, groups - 1 + RING - 1 + 2)

    def origin(i):
        hop = (i + 1) // 2
        return (z + jnp.where(i % 2 == 1, RING - hop, hop)) % RING

    def stream(kind):
        return (keys_all, 0) if kind == 0 else (values_all, 1)

    def ring_copy(kind, i, sem, ahead):
        buf, which = stream(kind)
        block = ctx_of(0 if kind == 2 else plane, origin(i), core)
        return remote(buf.at[block], buf.at[block], send_f.at[kind, sem], recv_kv.at[which, block],
                      ctx=ctx_of(plane, (z + jnp.where(ahead, 1, RING - 1)) % RING, core))

    def f_copy(kind, i):
        return ring_copy(kind, i, i, i % 2 == 1)

    def first_copy(kind, ahead):
        return ring_copy(kind, 0, 0 if ahead else RING - 1, ahead)

    def x_copy(kind, i):
        buf, which = stream(kind)
        block = ctx_of(0, origin(i), core)
        return remote(buf.at[block], buf.at[block], send_x.at[which, i], recv_kv.at[which, block],
                      ctx=ctx_of(1, z, core))

    def s_copy(kind, owner, i):
        buf, which = stream(kind)
        block = ctx_of(owner, origin(i), core)
        return remote(buf.at[block], buf.at[block], send_s.at[which, owner * RING + i],
                      recv_kv.at[which, block], ctx=ctx_of(plane, z, 1 - core))

    def g_copy(s):
        return remote(stage_g.at[s], landed_g.at[s], send_g.at[s], recv_g.at[s],
                      dp=(group + groups - s) % groups)

    def o_copy(s):
        return remote(stage_o.at[s], landed_o.at[s], send_o.at[s], recv_o.at[s],
                      dp=(group + s) % groups)

    def arrived(kind, block):
        buf, which = stream(kind)
        remote(buf.at[block], buf.at[block], send_f.at[0, 0], recv_kv.at[which, block],
               ctx=ctx_of(plane, z, 1 - core)).wait_recv()

    loop(1, groups, lambda s: g_copy(s).start())
    for kind in range(2):
        first_copy(kind, True).start()
        first_copy(kind, False).start()

        @pl.when(plane == 0)
        def _():
            x_copy(kind, 0).start()

        s_copy(kind, plane, 0).start()


    def fold(x):
        return x.reshape(x.shape[0] // 8, 8, x.shape[1])

    def score(n):
        keys = keys_all[pl.ds(CORES * n, CORES)].reshape(tile, HDIM)
        at = n * tile + lax.broadcasted_iota(jnp.int32, (tile, tok), 0)
        mine = ctx * tok + lax.broadcasted_iota(jnp.int32, (tile, tok), 1)
        bias = jnp.where((at >= starts_ref[...]) & (at <= mine), 0.0, MASKED)
        bias = jnp.concatenate([bias] * (wide // tok), axis=1)
        for c in chunks:
            s = dot(keys, qh[c], NT) + bias
            scores[n, :, c] = s
            top[:, c] = jnp.maximum(top[:, c], jnp.max(fold(s), axis=0))

    def gather_step(i):
        @pl.when((i >= 1) & (i < RING))
        def _():
            for kind in range(2):
                arrived(kind, ctx_of(plane, origin(i), core))

                @pl.when(i < RING - 2)
                def _():
                    f_copy(kind, i).start()

                if kind == 0:
                    @pl.when(plane == 0)
                    def _():
                        x_copy(0, i).start()

                s_copy(kind, plane, i).start()

        @pl.when((plane == 1) & (i >= 1) & (i <= RING))
        def _():
            j = i - 1
            for kind in (0, 2):
                arrived(kind, ctx_of(0, origin(j), core))
                if kind == 2:
                    @pl.when(j == 0)
                    def _():
                        first_copy(2, True).start()
                        first_copy(2, False).start()

                    @pl.when((j >= 1) & (j < RING - 2))
                    def _():
                        f_copy(2, j).start()

                s_copy(kind, 0, j).start()

        @pl.when((i >= 1) & (i <= RING))
        def _():
            near = plane * RING + origin(i - 1)
            arrived(0, CORES * near + 1 - core)

            @pl.when(near <= 2 * own_pair + 1)
            def _():
                score(near)

        @pl.when((plane == 1) & (i >= 2))
        def _():
            arrived(0, CORES * origin(i - 2) + 1 - core)
            score(origin(i - 2))

    loop(0, RING + 2, gather_step)
    top[...] = jnp.broadcast_to(jnp.max(top[...], axis=0, keepdims=True) * to_two, top.shape)

    loop(0, RING, lambda i: arrived(1, ctx_of(plane, i, 1 - core)))

    @pl.when(plane == 1)
    def _():
        loop(0, RING, lambda i: arrived(1, ctx_of(0, i, 1 - core)))

    def weigh(u):
        values = values_all[pl.ds(2 * CORES * u, 2 * CORES)].reshape(2 * tile, HDIM)
        for c in chunks:
            s = scores[pl.ds(2 * u, 2), :, c].reshape(2 * tile, wide)
            p = jnp.exp2(s * to_two - top[0:1, c])
            total[:, c] += jnp.sum(fold(p), axis=0)
            p = p.astype(jnp.bfloat16)
            probs[u, :, c] = p
            outT[:, c] += dot(values, p, TN)

    loop(0, own_pair + 1, weigh)
    inverse = 1.0 / jnp.sum(total[...], axis=0, keepdims=True)
    total[...] = jnp.broadcast_to(inverse, total.shape)
    for h in range(heads):
        mine = slice(h * tok, (h + 1) * tok)
        out = flip((outT[:, mine] * total[0:1, mine]).astype(jnp.bfloat16)).astype(jnp.bfloat16)
        attn[:, :, h * HDIM:(h + 1) * HDIM] = out.reshape(slots, block_rows, HDIM)
    for s in range(groups):
        block = attn[slot_of(plan_ref, s, slots)]
        if s == 0:
            landed_o[0] = block
        else:
            stage_o[s] = block
    loop(1, groups, lambda s: o_copy(s).start())

    loop(1, groups, lambda s: g_copy(s).wait_recv())
    for t in range(slots):
        block = landed_g[plan_ref[0, t]]
        for h in range(heads):
            first = h * tok + t * block_rows
            gh[first:first + block_rows] = block[:, h * HDIM:(h + 1) * HDIM]
    ones = jnp.ones((8, HDIM), jnp.bfloat16)
    for h in range(heads):
        mine = slice(h * tok, (h + 1) * tok)
        out = attn[:, :, h * HDIM:(h + 1) * HDIM].reshape(tok, HDIM)
        grad = gh[mine].astype(jnp.float32)
        prod = grad * out.astype(jnp.float32)
        high = prod.astype(jnp.bfloat16)
        low = (prod - high.astype(jnp.float32)).astype(jnp.bfloat16)
        dotT[:, mine] = dot(ones, high, NT) + dot(ones, low, NT)
        spread = jnp.broadcast_to(total[0:1, mine], (HDIM, tok))
        coarse = spread.astype(jnp.bfloat16)
        fine = (spread - coarse.astype(jnp.float32)).astype(jnp.bfloat16)
        back = flip(coarse) + flip(fine)
        gs[mine] = (grad * back).astype(jnp.bfloat16)
        qs[mine] = (qh[mine].astype(jnp.float32) * (back * scale)).astype(jnp.bfloat16)

    far = plane * (PAIRS // 2)

    near_pairs = z // 2 + 1

    def far_pair(turn):
        flip_way = (turn == 1) == (z // 2 % 2 == 0)
        step = jnp.where(turn == 0, 2, jnp.where(turn == 3, 0, jnp.where(flip_way, 1, 3)))
        return (z // 2 + step) % (PAIRS // 2)

    def pair_at(i):
        away = (plane == 1) & ((i % 2 == 0) | (i >= 2 * near_pairs))
        turn = jnp.where(i < 2 * near_pairs, i // 2, i - near_pairs)
        near = (2 * near_pairs - 2 - jnp.where(plane == 1, turn, i)) % near_pairs
        return jnp.where(away, far_pair(turn), far + near)

    def s2_copy(u):
        return remote(part.at[u, 1 - core], sib.at[u], send_s2.at[u], recv_s2.at[u],
                      ctx=ctx_of(plane, z, 1 - core))

    def x2_copy(spot):
        u, which = spot // 2, spot % 2
        return remote(pair.at[u, which], xbuf.at[u, which], send_x2.at[spot], recv_x2.at[spot],
                      ctx=ctx_of(1 - plane, z, core))

    def z2_copy(spot):
        return remote(pair.at[far + spot // 2, spot % 2], zbuf.at[z], send_z2.at[spot],
                      recv_z2.at[z], ctx=ctx_of(plane, spot, core))

    def back(u):
        keys = keys_all[pl.ds(2 * CORES * u, 2 * CORES)].reshape(2 * tile, HDIM)
        values = values_all[pl.ds(2 * CORES * u, 2 * CORES)].reshape(2 * tile, HDIM)
        dp = dot(values, gh[...], NT)
        p = probs[u]
        ds = (p.astype(jnp.float32) * (dp - dotT[0:1])).astype(jnp.bfloat16)
        dqT[...] += dot(keys, ds, TN)
        dk = dot(ds, qs[...], NN).astype(jnp.bfloat16)
        dv = dot(p, gs[...], NN).astype(jnp.bfloat16)
        for which in range(2):
            for c in range(CORES):
                first = (which * CORES + c) * tok
                part[u, c, which, :, :HDIM] = dk[first:first + tok]
                part[u, c, which, :, HDIM:] = dv[first:first + tok]

    def pass_on(u):
        s2_copy(u).wait_recv()
        pair[u] = add(part[u, core], sib[u])

        @pl.when(u < far)
        def _():
            x2_copy(2 * u).start()
            x2_copy(2 * u + 1).start()

        @pl.when((plane == 1) & (u >= far))
        def _():
            for which in range(2):
                spot = (u - far) * 2 + which

                @pl.when(spot < z)
                def _():
                    z2_copy(spot).start()

    def back_step(i):
        u = pair_at(i)
        back(u)
        s2_copy(u).start()

        @pl.when(i >= 1)
        def _():
            pass_on(pair_at(i - 1))

    loop(0, own_pair + 1, back_step)
    pass_on(pair_at(own_pair))

    for h in range(heads):
        mine = slice(h * tok, (h + 1) * tok)
        dq_ref[:, h * HDIM:(h + 1) * HDIM] = flip(
            (dqT[:, mine] * (total[0:1, mine] * scale)).astype(jnp.bfloat16)).astype(jnp.bfloat16)

    @pl.when(plane == 0)
    def _():
        def fold_in(j):
            u = far_pair(j)
            for which in range(2):
                spot = u * 2 + which
                x2_copy(spot).wait_recv()

                @pl.when(u <= own_pair)
                def _():
                    pair[u, which] = add(pair[u, which], xbuf[u, which])

                @pl.when(u > own_pair)
                def _():
                    pair[u, which] = xbuf[u, which]

                @pl.when(spot != z)
                def _():
                    z2_copy(spot).start()

        loop(0, PAIRS // 2, fold_in)

    acc[...] = pair[own_pair, z % 2].astype(jnp.float32)

    def z_land(s):
        source = (z + s) % RING

        @pl.when((plane == 0) | (source > z))
        def _():
            remote(zbuf.at[source], zbuf.at[source], send_z2.at[0], recv_z2.at[source],
                   ctx=ctx_of(plane, source, core)).wait_recv()
            acc[...] += zbuf[source].astype(jnp.float32)

    loop(1, RING, z_land)
    kg_ref[0] = acc[:, :HDIM].astype(jnp.bfloat16)
    vg_ref[0] = acc[:, HDIM:].astype(jnp.bfloat16)

    loop(1, groups, lambda s: o_copy(s).wait_recv())
    for t in range(slots):
        moved_ref[t] = landed_o[plan_ref[0, t]]

    def exchanged(s):
        g_copy(s).wait_send()
        o_copy(s).wait_send()

    loop(1, groups, exchanged)
    for kind in range(2):
        first_copy(kind, True).wait_send()
        first_copy(kind, False).wait_send()
        loop(1, RING - 2, lambda i: f_copy(kind, i).wait_send())

    @pl.when(plane == 0)
    def _():
        x_copy(1, 0).wait_send()

    @pl.when(plane == 1)
    def _():
        first_copy(2, True).wait_send()
        first_copy(2, False).wait_send()
        loop(1, RING - 2, lambda i: f_copy(2, i).wait_send())

    def gathered(i):
        for kind in range(2):
            s_copy(kind, plane, i).wait_send()

        @pl.when(plane == 0)
        def _():
            x_copy(0, i).wait_send()

        @pl.when(plane == 1)
        def _():
            s_copy(0, 0, i).wait_send()
            s_copy(1, 0, i).wait_send()

        @pl.when((i < z) | ((plane == 0) & (i != z)))
        def _():
            z2_copy(i).wait_send()

        @pl.when(plane == 1)
        def _():
            x2_copy(i).wait_send()

    loop(0, RING, gathered)
    loop(0, own_pair + 1, lambda i: s2_copy(pair_at(i)).wait_send())


def hand_over(moved_in, dq_in, kg_in, vg_in, moved_out, dq_out, kg_out, vg_out):
    moved_out[...] = moved_in[...]
    dq_out[...] = dq_in[...]
    kg_out[...] = kg_in[...]
    vg_out[...] = vg_in[...]


def per_device(queries, key_states, value_states, doc_start, move_plan, out_grad):
    tok, width = queries.shape[1:]
    heads = width // HDIM
    rows = heads * tok
    groups = lax.axis_size("dp")
    pieces = lax.axis_size("ctx")
    slots = move_plan.shape[1]
    block_rows = tok // slots
    tile = CORES * tok
    vmem = pl.BlockSpec(memory_space=pltpu.VMEM)
    smem = pl.BlockSpec(memory_space=pltpu.SMEM)
    bf, f32 = jnp.bfloat16, jnp.float32
    dma = pltpu.SemaphoreType.DMA
    blocks = pltpu.VMEM((groups, block_rows, width), bf)
    heads_bf = pltpu.VMEM((rows, HDIM), bf)

    moved, dq, kg, vg = pl.pallas_call(
        functools.partial(kernel, groups, slots, heads),
        out_shape=(
            jax.ShapeDtypeStruct((slots, block_rows, width), bf),
            jax.ShapeDtypeStruct((tok, width), bf),
            jax.ShapeDtypeStruct((1, tok, HDIM), bf),
            jax.ShapeDtypeStruct((1, tok, HDIM), bf),
        ),
        in_specs=[vmem, vmem, vmem, vmem, smem, vmem],
        out_specs=(vmem,) * 4,
        scratch_shapes=[
            pltpu.VMEM((pieces, tok, HDIM), bf),
            pltpu.VMEM((pieces, tok, HDIM), bf),
            pltpu.VMEM((tok, tok), bf),
            heads_bf, heads_bf, heads_bf, heads_bf,
            pltpu.VMEM((2 * PAIRS, tile, rows), f32),
            pltpu.VMEM((PAIRS, 2 * tile, rows), bf),
            pltpu.VMEM((8, rows), f32),
            pltpu.VMEM((8, rows), f32),
            pltpu.VMEM((HDIM, rows), f32),
            pltpu.VMEM((HDIM, rows), f32),
            pltpu.VMEM((8, rows), f32),
            pltpu.VMEM((slots, block_rows, width), bf),
            blocks, blocks, blocks, blocks,
            pltpu.VMEM((PAIRS, CORES, 2, tok, 2 * HDIM), bf),
            pltpu.VMEM((PAIRS, 2, tok, 2 * HDIM), bf),
            pltpu.VMEM((PAIRS, 2, tok, 2 * HDIM), bf),
            pltpu.VMEM((PAIRS // 2, 2, tok, 2 * HDIM), bf),
            pltpu.VMEM((RING, tok, 2 * HDIM), bf),
            pltpu.VMEM((tok, 2 * HDIM), f32),
            dma((3, RING)), dma((2, RING)), dma((2, 2 * RING)), dma((2, pieces)),
            dma((groups,)), dma((groups,)), dma((groups,)), dma((groups,)),
            dma((PAIRS,)), dma((PAIRS,)), dma((RING,)), dma((RING,)),
            dma((RING,)), dma((RING,)),
        ],
        compiler_params=pltpu.CompilerParams(
            collective_id=0, has_side_effects=True, vmem_limit_bytes=VMEM_LIMIT),
    )(
        queries[0], key_states, value_states, doc_start, move_plan,
        out_grad.reshape(slots, block_rows, width),
    )
    moved, dq, kg, vg = pl.pallas_call(
        hand_over,
        out_shape=tuple(jax.ShapeDtypeStruct(x.shape, x.dtype) for x in (moved, dq, kg, vg)),
        in_specs=[vmem] * 4,
        out_specs=(vmem,) * 4,
    )(moved, dq, kg, vg)
    return moved.reshape(1, tok, width), dq[None], kg, vg


def solution(mesh):
    split = P("dp", "ctx", None)
    return jax.shard_map(
        per_device,
        mesh=mesh,
        in_specs=(split, split, split, P("dp", "ctx"), P("ctx", None), split),
        out_specs=(split, split, split, split),
        check_vma=False,
    )
```
